128 devices in a mesh: freq: 32 (over x, z_hi, y), src: 4 (over z_lo, core).
Axes of the slice: x: 4, y: 4, z: 4 (z_hi: 2, z_lo: 2; z = z_hi * 2 + z_lo), core: 2. Of those that a mesh axis runs over, the one named last changes fastest.
Arguments:
- reflection: bfloat16 [2, 128, 2048, 2048], P(None, 'freq', None, 'src'), may hold values from -0.125 to 0.125
- aperture: int32 [16, 16], P(None, 'src'), may hold values 0 or 1
- initial: bfloat16 [2, 128, 128, 2048], P(None, 'freq', None, 'src'), may hold values from -6 to 6
- onsets: int32 [128, 2048], P('freq', 'src'), may hold values from 16 to 127
Outputs:
- focusing: bfloat16 [2, 128, 128, 2048], P(None, 'freq', None, 'src')
The draws below stay inside these ranges and needn't reach their ends.
All inputs are finite; a program needn't handle non-finite values. No bound on the sum of `aperture` on one device may be relied on, other than what follows from the above.
Results may differ from the reference program's by a relative error of at most 0.02.
Values may be sent and summed in bfloat16 or wider, within the bound.
No kernel may reach another device: no remote copies, remote signals or barrier semaphores. Data moves between devices by JAX's collectives and lax.ppermute only.
A program may use at most 128 MiB of HBM per device.

```python
import math
import jax
import jax.numpy as jnp
from jax import lax

NF = 128
NR = 2048
BLOCK = 128
NP = 128
ITERS = 2
NS_DEV = 512
N_SRC = 4


def touch_ends(drawn, rng, least, top_value):
    shape = drawn.shape
    place = [jax.random.randint(jax.random.fold_in(rng, axis), (), 0, shape[axis]) for axis in range(len(shape))]
    drawn = drawn.at[tuple(place)].set(least)
    longest = shape.index(max(shape))
    place[longest] = (place[longest] + 1) % shape[longest]
    return drawn.at[tuple(place)].set(top_value)


def block_levels(stream_key, dims, cuts, smallest, largest):
    factor_of, own = 1.0, jax.random.fold_in(stream_key, 6)
    for dim, parts in cuts:
        heights = jnp.exp(jax.random.uniform(jax.random.fold_in(own, dim), (parts,), jnp.float32, smallest / len(cuts), largest / len(cuts)))
        factor_of = factor_of * jnp.repeat(heights, dims[dim] // parts).reshape([-1 if axis == dim else 1 for axis in range(len(dims))])
    return factor_of


def centred(rng, extent, scale, most, split=(), kind=jnp.bfloat16):
    level = block_levels(rng, extent, split, -0.22, 0.18) if split else 1.0
    entries = jax.random.normal(rng, extent, jnp.float32) * scale * level
    return jnp.minimum(jnp.maximum(entries, -most), most).astype(kind)


def setup_inputs(seed: int = 0) -> dict:
    seeds = jax.random.split(jax.random.key(seed), 5)
    return {
        "reflection": centred(seeds[0], (2, NF, NR, NR), NR ** -0.5, 0.125, ((1, 32), (3, 4))),
        "aperture": touch_ends((jax.random.randint(seeds[1], (NR // BLOCK, NR // BLOCK), 0, 4) < 3).astype(jnp.int32), jax.random.fold_in(seeds[1], 1), 0, 1),
        "initial": centred(seeds[2], (2, NF, NP, NR), 1.0, 6.0, ((1, 32), (3, 4))),
        "onsets": touch_ends(jax.random.randint(seeds[3], (NP, NR), NF // 8, NF), jax.random.fold_in(seeds[3], 1), NF // 8, NF - 1).astype(jnp.int32),
    }


def precise(left, right):
    return jnp.dot(left, right, precision=lax.Precision.HIGHEST, preferred_element_type=jnp.float32)


def reference(reflection, aperture, initial, onsets):
    expanded = jnp.repeat(jnp.repeat(aperture, BLOCK, axis=0), BLOCK, axis=1).astype(jnp.bfloat16)
    positions = jnp.arange(NF, dtype=jnp.int32)
    phases = ((positions[:, None] * positions[None, :]) % NF).astype(jnp.float32) * (2.0 * math.pi / NF)
    cosine = jnp.cos(phases)
    sine = jnp.sin(phases)
    window = (positions[:, None, None] < onsets[None, :, :]).astype(jnp.float32).reshape(NF, NP * NR)
    current = initial
    for iteration in range(ITERS):
        polarity = 1.0 if iteration % 2 == 0 else -1.0

        def one_frequency(pieces):
            refl_real, refl_imag, focus_real, focus_imag = pieces
            refl_real = refl_real * expanded
            refl_imag = refl_imag * expanded
            run_real = jnp.zeros((NP, NR), jnp.float32)
            run_imag = jnp.zeros((NP, NR), jnp.float32)
            for group in range(N_SRC):
                lower = group * NS_DEV
                upper = lower + NS_DEV
                left_real = refl_real[:, lower:upper].astype(jnp.float32).T
                left_imag = refl_imag[:, lower:upper].astype(jnp.float32).T
                vec_real = focus_real[:, lower:upper].astype(jnp.float32)
                vec_imag = focus_imag[:, lower:upper].astype(jnp.float32)
                part_real = precise(vec_real, left_real) - polarity * precise(vec_imag, left_imag)
                part_imag = precise(vec_imag, left_real) + polarity * precise(vec_real, left_imag)
                part_real = lax.optimization_barrier(part_real.astype(jnp.bfloat16))
                part_imag = lax.optimization_barrier(part_imag.astype(jnp.bfloat16))
                run_real = run_real + part_real.astype(jnp.float32)
                run_imag = run_imag + part_imag.astype(jnp.float32)
            return run_real, run_imag

        resp_real, resp_imag = lax.map(one_frequency, (reflection[0], reflection[1], current[0], current[1]))
        flat_real = resp_real.reshape(NF, NP * NR)
        flat_imag = resp_imag.reshape(NF, NP * NR)
        time_real = (precise(cosine, flat_real) - precise(sine, flat_imag)) / NF
        time_imag = (precise(sine, flat_real) + precise(cosine, flat_imag)) / NF
        time_real = time_real * window
        time_imag = time_imag * window
        back_real = precise(cosine, time_real) + precise(sine, time_imag)
        back_imag = precise(cosine, time_imag) - precise(sine, time_real)
        spectra = jnp.stack([back_real, back_imag]).reshape(2, NF, NP, NR)
        current = (initial.astype(jnp.float32) + spectra).astype(jnp.bfloat16)
    return current
```

```python
import functools
import math

import jax
import jax.numpy as jnp
import numpy as np
from jax import lax
from jax.experimental import pallas as pl
from jax.experimental.pallas import tpu as pltpu
from jax.sharding import PartitionSpec as P

ITERS = 2
CHUNKS = 2
LIMIT = 48 * 1024 * 1024
NT = (((1,), (1,)), ((), ()))


def mm(left, right):
    return jnp.dot(left, right, preferred_element_type=jnp.float32)


def nt(left, right):
    return lax.dot_general(left, right, NT, preferred_element_type=jnp.float32)


def split(values):
    high = values.astype(jnp.bfloat16)
    low = (values - high.astype(values.dtype)).astype(jnp.bfloat16)
    return high, low


def tables(nfreq, freq_local, focal_block, chunks):
    devices = nfreq // freq_local
    sub = focal_block // chunks
    packed = nfreq * 2 * sub
    pack = np.zeros((packed, packed), np.float32)
    focal = devices * focal_block
    choose = np.zeros((chunks, devices * sub, focal), np.float32)
    place = np.zeros((2, freq_local, focal, chunks, packed), np.float32)
    for d in range(devices):
        for j in range(sub):
            for k in range(chunks):
                choose[k, d * sub + j, d * focal_block + k * sub + j] = 1
            for f in range(freq_local):
                for c in range(2):
                    row = ((d * freq_local + f) * 2 + c) * sub + j
                    pack[row, ((f * 2 + c) * devices + d) * sub + j] = 1
                    for k in range(chunks):
                        place[c, f, d * focal_block + k * sub + j, k, row] = 1
    positions = np.arange(nfreq)
    phase = (np.outer(positions, positions) % nfreq) * (2.0 * math.pi / nfreq)
    cosine, sine = np.cos(phase), np.sin(phase)
    eye = np.eye(sub)
    to_time = np.zeros((sub, 2, nfreq, nfreq, 2, sub))
    to_freq = np.zeros((nfreq, 2, sub, sub, 2, nfreq))
    for j in range(sub):
        to_time[j, 0, :, :, 0, j] = cosine / nfreq
        to_time[j, 0, :, :, 1, j] = -sine / nfreq
        to_time[j, 1, :, :, 0, j] = sine / nfreq
        to_time[j, 1, :, :, 1, j] = cosine / nfreq
        to_freq[:, 0, j, j, 0, :] = cosine
        to_freq[:, 0, j, j, 1, :] = sine
        to_freq[:, 1, j, j, 0, :] = -sine
        to_freq[:, 1, j, j, 1, :] = cosine
    to_time = to_time.reshape(packed, packed).astype(np.float32)
    to_freq = to_freq.reshape(packed, packed).astype(np.float32)
    return pack, choose, place, to_time, to_freq


def pair(matrix):
    high = matrix.astype(jnp.bfloat16)
    low = (matrix - high.astype(np.float32)).astype(jnp.bfloat16)
    return np.stack([high, low])


def product_kernel(polarity, chunk_rows, block, first, src_ref, mask_ref, choose_ref, initial_ref, *refs):
    if first:
        reflection_ref, *outs, left_ref, right_ref = refs
    else:
        unpack_ref, update_ref, reflection_ref, *outs, left_ref, right_ref = refs
    lo = pl.program_id(0)
    freq = pl.program_id(1)
    half = chunk_rows // 2
    chunks = len(outs)

    @pl.when(lo == 0)
    def _():
        planes = []
        for chunk in range(chunks):
            pick = choose_ref[chunk]
            for plane in range(2):
                value = mm(pick, initial_ref[plane, 0])
                if not first:
                    rows = unpack_ref[plane]
                    value = value + mm(rows, update_ref[...])
                planes.append(value)
        for chunk in range(chunks):
            real, imag = planes[2 * chunk], planes[2 * chunk + 1]
            base = chunk * chunk_rows
            left_ref[freq, base : base + half, :] = real.astype(jnp.bfloat16)
            left_ref[freq, base + half : base + chunk_rows, :] = imag.astype(jnp.bfloat16)
            right_ref[freq, base : base + half, :] = (-polarity * imag).astype(jnp.bfloat16)
            right_ref[freq, base + half : base + chunk_rows, :] = (polarity * real).astype(jnp.bfloat16)

    receivers = reflection_ref.shape[2]
    count = receivers // block
    row_block = jnp.bitwise_xor(src_ref[0], 2 * lo + src_ref[1])
    masked = []
    for plane in range(2):
        strips = []
        for strip in range(count):
            mask = mask_ref[pl.ds(row_block * count + strip, 1), :].astype(jnp.bfloat16)
            strips.append(reflection_ref[plane, 0, strip * block : (strip + 1) * block, :] * mask)
        masked.append(jnp.concatenate(strips, axis=0))
    total = nt(left_ref[freq], masked[0]) + nt(right_ref[freq], masked[1])
    for chunk in range(chunks):
        outs[chunk][0, 0] = total[chunk * chunk_rows : (chunk + 1) * chunk_rows].astype(jnp.bfloat16)


def products(reflection, mask, choose, initial, src, other_core, polarity, unpack=None, update=None):
    planes, nfreq, receivers, sources = reflection.shape
    chunks, half, focal = choose.shape
    rows = 2 * half
    first = update is None
    block = receivers // mask.shape[0]
    where = jnp.stack([src, jnp.full_like(src, int(other_core))])
    width = sources
    in_specs = [
        pl.BlockSpec(mask.shape, lambda l, f, s: (0, 0)),
        pl.BlockSpec(choose.shape, lambda l, f, s: (0, 0, 0)),
        pl.BlockSpec((2, 1, focal, sources), lambda l, f, s: (0, jnp.where(l == 0, f, nfreq - 1), 0, 0)),
    ]
    args = [mask, choose, initial]
    if not first:
        in_specs.append(
            pl.BlockSpec((None, 2, half, update.shape[0]), lambda l, f, s: (jnp.where(l == 0, f, nfreq - 1), 0, 0, 0))
        )
        in_specs.append(pl.BlockSpec(update.shape, lambda l, f, s: (0, 0)))
        args += [unpack, update]
    in_specs.append(
        pl.BlockSpec(
            (2, 1, width, sources),
            lambda l, f, s: (0, f, jnp.bitwise_xor(s[0], 2 * l + s[1]), 0),
        )
    )
    args.append(reflection)
    out = jax.ShapeDtypeStruct((2, nfreq, rows, width), jnp.bfloat16)
    return pl.pallas_call(
        functools.partial(product_kernel, polarity, rows, block, first),
        grid_spec=pltpu.PrefetchScalarGridSpec(
            num_scalar_prefetch=1,
            grid=(2, nfreq),
            in_specs=in_specs,
            out_specs=[pl.BlockSpec((1, 1, rows, width), lambda l, f, s: (l, f, 0, 0))] * chunks,
            scratch_shapes=[
                pltpu.VMEM((nfreq, chunks * rows, sources), jnp.bfloat16),
                pltpu.VMEM((nfreq, chunks * rows, sources), jnp.bfloat16),
            ],
        ),
        out_shape=[out] * chunks,
        compiler_params=pltpu.CompilerParams(vmem_limit_bytes=LIMIT),
        cost_estimate=pl.CostEstimate(
            flops=2 * 2 * nfreq * 2 * 256 * width * sources, bytes_accessed=reflection.size, transcendentals=0
        ),
        name="products",
    )(where, *args)


def whole(kernel, shape, flops, name, *args):
    return pl.pallas_call(
        kernel,
        out_shape=jax.ShapeDtypeStruct(shape, jnp.bfloat16),
        compiler_params=pltpu.CompilerParams(vmem_limit_bytes=LIMIT),
        cost_estimate=pl.CostEstimate(flops=flops, bytes_accessed=2 * 512 * 1024, transcendentals=0),
        name=name,
    )(*args)


def pack_kernel(pack_ref, mine_ref, core_ref, far_ref, out_ref):
    total = mine_ref[...].astype(jnp.float32) + core_ref[...].astype(jnp.float32)
    total = (total + far_ref[...].astype(jnp.float32)).astype(jnp.bfloat16)
    out_ref[...] = mm(pack_ref[...], total).astype(jnp.bfloat16)


def window_kernel(sub, to_time_ref, to_freq_ref, onsets_ref, traces_ref, out_ref):
    traces = traces_ref[...]
    time = mm(to_time_ref[0], traces) + mm(to_time_ref[1], traces)
    nfreq = time.shape[0] // (2 * sub)
    step = lax.broadcasted_iota(jnp.int32, (nfreq, time.shape[1]), 0)
    parts = []
    for j in range(sub):
        keep = step < onsets_ref[j : j + 1, :]
        for plane in range(2):
            base = (j * 2 + plane) * nfreq
            parts.append(jnp.where(keep, time[base : base + nfreq], 0.0))
    high, low = split(jnp.concatenate(parts, axis=0))
    back = mm(to_freq_ref[0], high) + mm(to_freq_ref[0], low) + mm(to_freq_ref[1], high)
    out_ref[...] = back.astype(jnp.bfloat16)


def final_kernel(place_ref, initial_ref, *refs):
    *updates, out_ref = refs
    value = initial_ref[0].astype(jnp.float32)
    for chunk, update in enumerate(updates):
        value = value + mm(place_ref[0, chunk], update[...])
    out_ref[0] = value.astype(jnp.bfloat16)


def finish(place, initial, updates):
    planes, nfreq, focal, sources = initial.shape
    flat = initial.reshape(planes * nfreq, focal, sources)
    out = pl.pallas_call(
        final_kernel,
        grid=(planes * nfreq,),
        in_specs=[
            pl.BlockSpec((1,) + place.shape[1:], lambda i: (i, 0, 0, 0)),
            pl.BlockSpec((1, focal, sources), lambda i: (i, 0, 0)),
        ]
        + [pl.BlockSpec(updates[0].shape, lambda i: (0, 0))] * len(updates),
        out_specs=pl.BlockSpec((1, focal, sources), lambda i: (i, 0, 0)),
        out_shape=jax.ShapeDtypeStruct(flat.shape, jnp.bfloat16),
        compiler_params=pltpu.CompilerParams(vmem_limit_bytes=LIMIT),
        name="finish",
    )(place, flat, *updates)
    return out.reshape(initial.shape)


def swap(values, bit):
    return lax.ppermute(values, "src", [(i, i ^ bit) for i in range(lax.axis_size("src"))])


def local(reflection, aperture, initial, onsets):
    planes, freq_local, receivers, sources = reflection.shape
    devices = lax.axis_size("freq")
    nfreq = freq_local * devices
    focal = initial.shape[2]
    focal_block = focal // devices
    sub = focal_block // CHUNKS
    block = receivers // aperture.shape[0]
    packed = nfreq * 2 * sub
    pack, choose, place, to_time, to_freq = tables(nfreq, freq_local, focal_block, CHUNKS)
    bf = jnp.bfloat16
    unpack = jnp.asarray(pack.T.reshape(freq_local, 2, devices * sub, packed), bf)
    pack = jnp.asarray(pack, bf)
    choose = jnp.asarray(choose, bf)
    place = jnp.asarray(
        place.reshape(2 * freq_local, focal, CHUNKS, packed).transpose(0, 2, 1, 3), bf
    )
    to_time = jnp.asarray(pair(to_time))
    to_freq = jnp.asarray(pair(to_freq))
    src = lax.axis_index("src").astype(jnp.int32)
    mask = jnp.repeat(aperture, block, axis=1).astype(jnp.float32)
    cost = 2 * packed * packed * sources

    def reduce_stage(keep, send):
        got = swap(send, 1)
        far = swap((keep[1].astype(jnp.float32) + got[1].astype(jnp.float32)).astype(bf), 2)
        shape = (packed, sources)
        return whole(
            pack_kernel, shape, cost, "pack", pack, keep[0].reshape(shape), got[0].reshape(shape), far.reshape(shape)
        )

    def transpose(values):
        blocks = values.reshape(devices, packed // devices, sources)
        return lax.all_to_all(blocks, "freq", 0, 0, tiled=True).reshape(packed, sources)

    updates = [None] * CHUNKS
    for iteration in range(ITERS):
        polarity = 1.0 if iteration % 2 == 0 else -1.0
        if iteration == 0:
            send = products(reflection, mask, choose, initial, src, True, polarity)
            keep = products(reflection, mask, choose, initial, src, False, polarity)
        for chunk in range(CHUNKS):
            if iteration == 0:
                mine, other = keep[chunk], send[chunk]
            else:
                pick = choose[chunk : chunk + 1]
                (other,) = products(reflection, mask, pick, initial, src, True, polarity, unpack, updates[chunk])
                (mine,) = products(reflection, mask, pick, initial, src, False, polarity, unpack, updates[chunk])
            response = transpose(reduce_stage(mine, other))
            limits = onsets[chunk * sub : (chunk + 1) * sub]
            truncated = whole(
                functools.partial(window_kernel, sub),
                (packed, sources),
                5 * cost,
                "window",
                to_time,
                to_freq,
                limits,
                response,
            )
            updates[chunk] = transpose(truncated)
    return finish(place, initial, updates)


def solution(mesh):
    placed = (
        P(None, "freq", None, "src"),
        P(None, "src"),
        P(None, "freq", None, "src"),
        P("freq", "src"),
    )
    return jax.shard_map(
        local, mesh=mesh, in_specs=placed, out_specs=P(None, "freq", None, "src"), check_vma=False
    )
```

```python
import functools
import math

import jax
import jax.numpy as jnp
import numpy as np
from jax import lax
from jax.experimental import pallas as pl
from jax.experimental.pallas import tpu as pltpu
from jax.sharding import PartitionSpec as P

ITERS = 2
AHEAD = 4
TOGETHER = 2
LANES = 128
MIB = 1024 * 1024
NT = (((1,), (1,)), ((), ()))
VMEM = pl.BlockSpec(memory_space=pltpu.VMEM)
BF = jnp.bfloat16
LIGHT = pl.CostEstimate(flops=1, bytes_accessed=1, transcendentals=0)


def mm(left, right):
    return jnp.dot(left, right, preferred_element_type=jnp.float32)


def nt(left, right):
    return lax.dot_general(left, right, NT, preferred_element_type=jnp.float32)


def split(values):
    high = values.astype(BF)
    low = (values - high.astype(values.dtype)).astype(BF)
    return high, low


def tables(columns, rows, freq_local, focal_block):
    plane_devices = columns * rows
    half = plane_devices * focal_block
    nfreq = 2 * plane_devices * freq_local
    packed = half * freq_local * 2
    pack = np.zeros((packed, packed), np.float32)
    for xy in range(plane_devices):
        for j in range(focal_block):
            for f in range(freq_local):
                for c in range(2):
                    row = ((xy * focal_block + j) * freq_local + f) * 2 + c
                    pack[row, ((f * 2 + c) * plane_devices + xy) * focal_block + j] = 1
    focal = np.arange(2 * half).reshape(columns, 2, rows * focal_block).transpose(1, 0, 2).reshape(2, half)
    choose = (focal[:, :, None] == np.arange(2 * half)).astype(np.float32)
    positions = np.arange(nfreq)
    phase = (np.outer(positions, positions) % nfreq) * (2.0 * math.pi / nfreq)
    cosine, sine = np.cos(phase), np.sin(phase)
    to_time = np.zeros((2, nfreq, nfreq, 2))
    to_time[0, :, :, 0] = cosine / nfreq
    to_time[0, :, :, 1] = -sine / nfreq
    to_time[1, :, :, 0] = sine / nfreq
    to_time[1, :, :, 1] = cosine / nfreq
    to_freq = np.zeros((nfreq, 2, 2, nfreq))
    to_freq[:, 0, 0, :] = cosine
    to_freq[:, 0, 1, :] = sine
    to_freq[:, 1, 0, :] = -sine
    to_freq[:, 1, 1, :] = cosine
    to_time = to_time.reshape(2 * nfreq, columns, 2, rows, freq_local * 2).transpose(0, 1, 3, 2, 4)
    to_time = to_time.reshape(2 * nfreq, 2 * nfreq).astype(np.float32)
    to_freq = to_freq.reshape(2 * nfreq, 2 * nfreq).astype(np.float32)
    return pack, choose, to_time, to_freq


def pair(matrix):
    high = matrix.astype(BF)
    low = (matrix - high.astype(np.float32)).astype(BF)
    return np.stack([high, low])


def spread(wide_ref, update_ref):
    for slab in range(wide_ref.shape[0]):
        wide_ref[slab] = update_ref[:, slab * LANES : (slab + 1) * LANES].astype(jnp.float32)


def every(wide_ref, start, count, stride):
    slabs = [wide_ref[slab, pl.ds(start, count, stride), :] for slab in range(wide_ref.shape[0])]
    return jnp.concatenate(slabs, axis=1)


def wide(update):
    rows, width = update.shape
    return pltpu.VMEM((width // LANES, rows, LANES), jnp.float32)


def weights(polarity, half, choose_ref, initial_ref, update_ref, wide_ref, left_ref, right_ref):
    nfreq = left_ref.shape[0]
    halves, count, focal = choose_ref.shape
    if update_ref is not None:
        spread(wide_ref, update_ref)
    for freq in range(nfreq):
        planes = []
        for plane in range(2):
            value = initial_ref[plane, freq]
            if update_ref is not None:
                update = every(wide_ref, 2 * freq + plane, focal, 2 * nfreq)
                value = (value.astype(jnp.float32) + update).astype(BF)
            planes.append(value)
        for place in range(halves):
            pick = choose_ref[jnp.bitwise_xor(half, place)]
            real, imag = mm(pick, planes[0]), mm(pick, planes[1])
            low = place * 2 * count
            left_ref[freq, :, low : low + 2 * count] = jnp.concatenate([real, imag], axis=0).T.astype(BF)
            right = jnp.concatenate([-polarity * imag, polarity * real], axis=0)
            right_ref[freq, :, low : low + 2 * count] = right.T.astype(BF)


def product_kernel(polarity, rels, build, tokens, src_ref, mask_ref, reflection_ref, *refs):
    update_ref = wide_ref = None
    if build == "first":
        choose_ref, initial_ref, *refs = refs
    elif build == "update":
        choose_ref, initial_ref, update_ref, *refs = refs
    else:
        left_ref, right_ref, *refs = refs
    refs = refs[tokens:]
    outs, refs = refs[: len(rels)], refs[len(rels) :]
    if build:
        left_ref, right_ref, *refs = refs
    held_ref, sems, *refs = refs
    if build == "update":
        (wide_ref,) = refs
    nfreq, width, _ = outs[0].shape
    pieces = [(place, freq) for place in range(len(rels)) for freq in range(nfreq)]
    source = src_ref[0]

    def fetch(piece, plane):
        place, freq = pieces[piece]
        block = jnp.bitwise_xor(source, rels[place])
        return pltpu.make_async_copy(
            reflection_ref.at[plane, freq, pl.ds(block * width, width), :],
            held_ref.at[piece, plane],
            sems.at[piece, plane],
        )

    def begin(piece):
        if piece < len(pieces):
            for plane in range(2):
                fetch(piece, plane).start()

    for piece in range(AHEAD):
        begin(piece)
    if build:
        weights(polarity, src_ref[1], choose_ref, initial_ref, update_ref, wide_ref, left_ref, right_ref)

    rows, pack = mask_ref.shape[0] // 4, mask_ref.shape[1]
    tall = width // rows
    for low in range(0, len(pieces), TOGETHER):
        both = range(low, min(low + TOGETHER, len(pieces)))
        for piece in both:
            for plane in range(2):
                fetch(piece, plane).wait()
        for piece in both:
            begin(piece + AHEAD)
        for piece in both:
            place, freq = pieces[piece]
            masked = []
            for plane in range(2):
                strips = []
                for strip in range(rows):
                    mask = mask_ref[jnp.bitwise_xor(source, rels[place]) * rows + strip]
                    part = held_ref[piece, plane, strip * tall : (strip + 1) * tall, :]
                    part = part.reshape(tall // pack, pack, part.shape[1]) * mask[None]
                    strips.append(part.reshape(tall, part.shape[2]))
                masked.append(jnp.concatenate(strips, axis=0))
            total = mm(masked[0], left_ref[freq]) + mm(masked[1], right_ref[freq])
            outs[place][freq] = total.astype(BF)


def products(polarity, rels, src, mask, reflection, choose, initial=None, update=None, built=None, after=()):
    planes, nfreq, receivers, sources = reflection.shape
    halves, half, focal = choose.shape
    lanes = 2 * half * halves
    out = jax.ShapeDtypeStruct((nfreq, sources, lanes), BF)
    scratch = [
        pltpu.VMEM((len(rels) * nfreq, 2, sources, sources), BF),
        pltpu.SemaphoreType.DMA((len(rels) * nfreq, 2)),
    ]
    outs = [out] * len(rels)
    if built is not None:
        build, extra = "", list(built)
    elif update is None:
        build, extra = "first", [choose, initial]
    else:
        build, extra = "update", [choose, initial, update]
        scratch.append(wide(update))
    if build:
        outs += [out] * 2
    anywhere = pl.BlockSpec(memory_space=pl.ANY)
    return pl.pallas_call(
        functools.partial(product_kernel, polarity, rels, build, len(after)),
        in_specs=[pl.BlockSpec(memory_space=pltpu.SMEM), VMEM, anywhere]
        + [VMEM] * len(extra)
        + [anywhere] * len(after),
        out_specs=[VMEM] * len(outs),
        scratch_shapes=scratch,
        out_shape=outs,
        compiler_params=pltpu.CompilerParams(vmem_limit_bytes=46 * MIB),
        cost_estimate=LIGHT,
        name="products",
    )(src, mask, reflection, *extra, *after)


def call(kernel, name, outs, *args, after=()):
    return pl.pallas_call(
        kernel,
        in_specs=[VMEM] * len(args) + [pl.BlockSpec(memory_space=pl.ANY)] * len(after),
        out_specs=[VMEM] * len(outs),
        out_shape=[jax.ShapeDtypeStruct(shape, BF) for shape in outs],
        compiler_params=pltpu.CompilerParams(vmem_limit_bytes=16 * MIB),
        cost_estimate=LIGHT,
        name=name,
    )(*args, *after)


def add_kernel(place, mine_ref, core_ref, out_ref):
    lanes = out_ref.shape[2]
    here = slice(place * lanes, (place + 1) * lanes)
    total = mine_ref[:, :, here].astype(jnp.float32) + core_ref[:, :, here].astype(jnp.float32)
    out_ref[...] = total.astype(BF)


def packed_sum(place, pack_ref, mine_ref, core_ref, far_ref):
    nfreq, width, lanes = far_ref.shape
    here = slice(place * lanes, (place + 1) * lanes)
    parts = []
    for f in range(nfreq):
        total = mine_ref[f, :, here].astype(jnp.float32) + core_ref[f, :, here].astype(jnp.float32)
        parts.append((total + far_ref[f].astype(jnp.float32)).astype(BF))
    return nt(pack_ref[...], jnp.concatenate(parts, axis=1)).astype(BF)


def pack_other_kernel(pack_ref, mine_ref, core_ref, far_ref, *refs):
    out_ref = refs[-1]
    out_ref[...] = packed_sum(1, pack_ref, mine_ref, core_ref, far_ref).reshape(out_ref.shape)


def pack_own_kernel(where_ref, pack_ref, mine_ref, core_ref, far_ref, outer_ref, out_ref):
    devices, rows, width = outer_ref.shape
    half = where_ref[1]
    own = packed_sum(0, pack_ref, mine_ref, core_ref, far_ref).reshape(outer_ref.shape)
    out_ref[:, pl.ds(pl.multiple_of(half * rows, rows), rows), :] = own
    out_ref[:, pl.ds(pl.multiple_of((1 - half) * rows, rows), rows), :] = outer_ref[...]


def pack_own(where, *args):
    devices, rows, width = args[-1].shape
    return pl.pallas_call(
        pack_own_kernel,
        in_specs=[pl.BlockSpec(memory_space=pltpu.SMEM)] + [VMEM] * len(args),
        out_specs=VMEM,
        out_shape=jax.ShapeDtypeStruct((devices, 2 * rows, width), BF),
        compiler_params=pltpu.CompilerParams(vmem_limit_bytes=16 * MIB),
        cost_estimate=LIGHT,
        name="pack_own",
    )(where, *args)


def window_kernel(dft_ref, onsets_ref, traces_ref, out_ref):
    focal, width = onsets_ref.shape
    devices, rows, _ = traces_ref.shape
    group = rows // (2 * focal)
    nfreq = dft_ref.shape[1] // 2
    step = lax.broadcasted_iota(jnp.int32, (nfreq, width), 0)
    traces = traces_ref[...].astype(jnp.float32).reshape(2 * devices, focal, group, width)
    results = []
    for j in range(focal):
        column = traces[:, j].reshape(2 * nfreq, width).astype(BF)
        time = mm(dft_ref[0], column) + mm(dft_ref[1], column)
        keep = step < onsets_ref[j : j + 1, :]
        keep = jnp.concatenate([keep, keep], axis=0)
        high, low = split(jnp.where(keep, time, 0.0))
        back = mm(dft_ref[2], high) + mm(dft_ref[2], low) + mm(dft_ref[3], high)
        results.append(back.reshape(2 * devices, group, width))
    out_ref[...] = jnp.stack(results, axis=1).reshape(out_ref.shape).astype(BF)


def final_kernel(initial_ref, update_ref, out_ref, wide_ref, block_ref, sems):
    planes, nfreq, focal, _ = initial_ref.shape
    spread(wide_ref, update_ref)
    copies = []
    for freq in range(nfreq):
        for plane in range(planes):
            value = initial_ref[plane, freq].astype(jnp.float32)
            value = value + every(wide_ref, planes * freq + plane, focal, planes * nfreq)
            block_ref[plane, freq] = value.astype(BF)
            copy = pltpu.make_async_copy(
                block_ref.at[plane, freq], out_ref.at[plane, freq], sems.at[plane, freq]
            )
            copy.start()
            copies.append(copy)
    for copy in copies:
        copy.wait()


def finish(initial, update):
    planes, nfreq, focal, sources = initial.shape
    return pl.pallas_call(
        final_kernel,
        in_specs=[VMEM, VMEM],
        out_specs=pl.BlockSpec(memory_space=pl.ANY),
        scratch_shapes=[
            wide(update),
            pltpu.VMEM(initial.shape, BF),
            pltpu.SemaphoreType.DMA((planes, nfreq)),
        ],
        out_shape=jax.ShapeDtypeStruct(initial.shape, BF),
        compiler_params=pltpu.CompilerParams(vmem_limit_bytes=16 * MIB),
        name="finish",
    )(initial, update)


def swap(values, bit):
    return lax.ppermute(values, "src", [(i, i ^ bit) for i in range(lax.axis_size("src"))])


def outward(values, columns, rows):
    pairs = []
    for x in range(columns):
        for h in range(2):
            for y in range(rows):
                for s in range(4):
                    here = ((x * 2 + h) * rows + y) * 4 + s
                    there = ((x * 2 + 1 - h) * rows + y) * 4 + (s ^ 2)
                    pairs.append((here, there))
    return lax.ppermute(values, ("freq", "src"), pairs)


def local(reflection, aperture, initial, onsets):
    planes, freq_local, receivers, sources = reflection.shape
    devices = lax.axis_size("freq")
    focal = initial.shape[2]
    focal_block = focal // devices
    block = receivers // aperture.shape[0]
    columns = rows = math.isqrt(devices // 2)
    pack, choose, to_time, to_freq = tables(columns, rows, freq_local, focal_block)
    pack = jnp.asarray(pack, BF)
    choose = jnp.asarray(choose, BF)
    dft = jnp.asarray(np.concatenate([pair(to_time), pair(to_freq)]))
    half = (lax.axis_index("freq") // rows) % 2
    where = jnp.stack([lax.axis_index("src"), half]).astype(jnp.int32)
    mask = jnp.repeat(aperture.astype(BF), block, axis=1)
    mask = jnp.broadcast_to(mask[:, None], (mask.shape[0], 16, sources))
    plane_groups = [
        [(x * 2 + h) * rows + y for x in range(columns) for y in range(rows)] for h in range(2)
    ]
    block_rows = focal_block * freq_local * planes
    part = (freq_local, sources, focal * planes // 2)

    update = None
    for iteration in range(ITERS):
        polarity = 1.0 if iteration % 2 == 0 else -1.0

        def respond(rel, **more):
            return products(polarity, (rel,), where, mask, reflection, choose, **more)

        send, left, right = respond(1, initial=initial, update=update)
        core_near = swap(send, 1)
        (near,) = respond(0, built=(left, right))
        (total,) = call(functools.partial(add_kernel, 1), "add", [part], near, core_near)
        far_other = swap(total, 2)
        (send,) = respond(3, built=(left, right), after=(total,))
        core_far = swap(send, 1)
        (remote,) = respond(2, built=(left, right), after=(total,))
        (total,) = call(functools.partial(add_kernel, 0), "add", [part], remote, core_far)
        far_own = swap(total, 2)
        shape = (devices // 2, block_rows, sources)
        (other,) = call(pack_other_kernel, "pack_other", [shape], pack, remote, core_far, far_other, after=(total,))
        outer = outward(other, columns, rows)
        responses = pack_own(where, pack, near, core_near, far_own, outer)
        traces = lax.all_to_all(responses, "freq", 0, 0, tiled=True, axis_index_groups=plane_groups)
        (truncated,) = call(
            window_kernel, "window", [(devices, block_rows, sources)], dft, onsets, traces
        )
        update = lax.all_to_all(truncated, "freq", 0, 0, tiled=True)
        update = update.reshape(devices * block_rows, sources)
    return finish(initial, update)


def solution(mesh):
    placed = (
        P(None, "freq", None, "src"),
        P(None, "src"),
        P(None, "freq", None, "src"),
        P("freq", "src"),
    )
    return jax.shard_map(
        local, mesh=mesh, in_specs=placed, out_specs=P(None, "freq", None, "src"), check_vma=False
    )
```

```python
import functools
import math

import jax
import jax.numpy as jnp
import numpy as np
from jax import lax
from jax.experimental import pallas as pl
from jax.experimental.pallas import tpu as pltpu
from jax.sharding import PartitionSpec as P

ITERS = 2
AHEAD = 4
TOGETHER = 2
CUTS = 2
TILE = 16
LANES = 128
MIB = 1024 * 1024
NT = (((1,), (1,)), ((), ()))
VMEM = pl.BlockSpec(memory_space=pltpu.VMEM)
BF = jnp.bfloat16
LIGHT = pl.CostEstimate(flops=1, bytes_accessed=1, transcendentals=0)


def mm(left, right):
    return jnp.dot(left, right, preferred_element_type=jnp.float32)


def nt(left, right):
    return lax.dot_general(left, right, NT, preferred_element_type=jnp.float32)


def split(values):
    high = values.astype(BF)
    low = (values - high.astype(values.dtype)).astype(BF)
    return high, low


def tables(columns, rows, freq_local, focal_block):
    plane_devices = columns * rows
    half = plane_devices * focal_block
    nfreq = 2 * plane_devices * freq_local
    packed = half * freq_local * 2
    pack = np.zeros((packed, packed), np.float32)
    for xy in range(plane_devices):
        for j in range(focal_block):
            for f in range(freq_local):
                for c in range(2):
                    row = ((xy * focal_block + j) * freq_local + f) * 2 + c
                    pack[row, ((f * 2 + c) * plane_devices + xy) * focal_block + j] = 1
    positions = np.arange(nfreq)
    phase = (np.outer(positions, positions) % nfreq) * (2.0 * math.pi / nfreq)
    cosine, sine = np.cos(phase), np.sin(phase)
    to_time = np.zeros((2, nfreq, nfreq, 2))
    to_time[0, :, :, 0] = cosine / nfreq
    to_time[0, :, :, 1] = -sine / nfreq
    to_time[1, :, :, 0] = sine / nfreq
    to_time[1, :, :, 1] = cosine / nfreq
    to_freq = np.zeros((nfreq, 2, 2, nfreq))
    to_freq[:, 0, 0, :] = cosine
    to_freq[:, 0, 1, :] = sine
    to_freq[:, 1, 0, :] = -sine
    to_freq[:, 1, 1, :] = cosine
    to_time = to_time.reshape(2 * nfreq, columns, 2, rows, freq_local * 2).transpose(0, 1, 3, 2, 4)
    to_time = to_time.reshape(2 * nfreq, 2 * nfreq).astype(np.float32)
    to_freq = to_freq.reshape(2 * nfreq, 2 * nfreq).astype(np.float32)
    return pack, to_time, to_freq


def pair(matrix):
    high = matrix.astype(BF)
    low = (matrix - high.astype(np.float32)).astype(BF)
    return np.stack([high, low])


def spread(wide_ref, update_ref):
    for slab in range(wide_ref.shape[0]):
        wide_ref[slab] = update_ref[:, slab * LANES : (slab + 1) * LANES].astype(jnp.float32)


def every(wide_ref, start, count, stride):
    slabs = [wide_ref[slab, pl.ds(start, count, stride), :] for slab in range(wide_ref.shape[0])]
    return jnp.concatenate(slabs, axis=1)


def wide(update):
    rows, width = update.shape
    return pltpu.VMEM((width // LANES, rows, LANES), jnp.float32)


def weights(polarity, half, block, initial_ref, update_ref, wide_ref, left_ref, right_ref):
    _, nfreq, focal, width = initial_ref.shape
    if update_ref is not None:
        spread(wide_ref, update_ref)
    for freq in range(nfreq):
        planes = []
        for plane in range(2):
            value = initial_ref[plane, freq].astype(jnp.float32)
            if update_ref is not None:
                value = value + every(wide_ref, 2 * freq + plane, focal, 2 * nfreq)
                value = value.astype(BF).astype(jnp.float32)
            value = value.reshape(focal // (2 * block), 2, block, width)
            planes.append([value[:, h].reshape(focal // 2, width) for h in range(2)])
        for place in range(2):
            real, imag = [jnp.where(half == place, low, high) for low, high in planes]
            here = slice(place * focal, (place + 1) * focal)
            left_ref[freq, :, here] = jnp.concatenate([real, imag], axis=0).T.astype(BF)
            right = jnp.concatenate([-polarity * imag, polarity * real], axis=0)
            right_ref[freq, :, here] = right.T.astype(BF)


def product_kernel(polarity, rels, build, tokens, focal_rows, where_ref, aperture_ref, reflection_ref, *refs):
    update_ref = wide_ref = None
    if build == "first":
        source_ref, *refs = refs
    elif build == "update":
        source_ref, update_ref, *refs = refs
    else:
        left_ref, right_ref, *refs = refs
    refs = refs[tokens:]
    outs, refs = refs[: len(rels)], refs[len(rels) :]
    if build:
        left_ref, right_ref, *refs = refs
    held_ref, sems, *refs = refs
    if build:
        initial_ref, initial_sem, *refs = refs
    if build == "update":
        (wide_ref,) = refs
    nfreq, width, _ = outs[0].shape
    pieces = [(place, freq) for place in range(len(rels)) for freq in range(nfreq)]
    blocks = [jnp.bitwise_xor(where_ref[0], rel) for rel in rels]

    def fetch(piece, plane):
        place, freq = pieces[piece]
        return pltpu.make_async_copy(
            reflection_ref.at[plane, freq, pl.ds(blocks[place] * width, width), :],
            held_ref.at[piece, plane],
            sems.at[piece, plane],
        )

    def begin(piece):
        if piece < len(pieces):
            for plane in range(2):
                fetch(piece, plane).start()

    if build:
        load = pltpu.make_async_copy(source_ref, initial_ref, initial_sem)
        load.start()
    for piece in range(AHEAD):
        begin(piece)
    if build:
        load.wait()
        weights(polarity, where_ref[1], focal_rows, initial_ref, update_ref, wide_ref, left_ref, right_ref)

    source_blocks, receiver_blocks = aperture_ref.shape
    strips = receiver_blocks // 4
    tall = width // strips
    wide_block = width // source_blocks

    def mask_of(place, strip):
        row = blocks[place] * strips + strip
        parts = [
            jnp.full((TILE, wide_block), aperture_ref[column, row].astype(jnp.float32)) for column in range(source_blocks)
        ]
        return jnp.concatenate(parts, axis=1).astype(BF)

    for low in range(0, len(pieces), TOGETHER):
        both = range(low, min(low + TOGETHER, len(pieces)))
        for piece in both:
            for plane in range(2):
                fetch(piece, plane).wait()
        for piece in both:
            begin(piece + AHEAD)
        for piece in both:
            place, freq = pieces[piece]
            masks = [mask_of(place, strip) for strip in range(strips)]
            masked = []
            for plane in range(2):
                parts = []
                for strip in range(strips):
                    part = held_ref[piece, plane, strip * tall : (strip + 1) * tall, :]
                    part = part.reshape(tall // TILE, TILE, width) * masks[strip][None]
                    parts.append(part.reshape(tall, width))
                masked.append(jnp.concatenate(parts, axis=0))
            total = mm(masked[0], left_ref[freq]) + mm(masked[1], right_ref[freq])
            outs[place][freq] = total.astype(BF)


def products(polarity, rels, focal_rows, where, aperture, reflection, initial, update=None, built=None, after=()):
    planes, nfreq, receivers, sources = reflection.shape
    focal = initial.shape[2]
    out = jax.ShapeDtypeStruct((nfreq, sources, 2 * focal), BF)
    scratch = [
        pltpu.VMEM((len(rels) * nfreq, 2, sources, sources), BF),
        pltpu.SemaphoreType.DMA((len(rels) * nfreq, 2)),
    ]
    outs = [out] * len(rels)
    anywhere = pl.BlockSpec(memory_space=pl.ANY)
    smem = pl.BlockSpec(memory_space=pltpu.SMEM)
    if built is not None:
        build, extra, specs = "", list(built), [VMEM] * 2
    else:
        outs += [out] * 2
        scratch += [pltpu.VMEM(initial.shape, BF), pltpu.SemaphoreType.DMA(())]
        if update is None:
            build, extra, specs = "first", [initial], [anywhere]
        else:
            build, extra, specs = "update", [initial, update], [anywhere, VMEM]
            scratch.append(wide(update))
    return pl.pallas_call(
        functools.partial(product_kernel, polarity, rels, build, len(after), focal_rows),
        in_specs=[smem, smem, anywhere] + specs + [anywhere] * len(after),
        out_specs=[VMEM] * len(outs),
        scratch_shapes=scratch,
        out_shape=outs,
        compiler_params=pltpu.CompilerParams(vmem_limit_bytes=46 * MIB),
        cost_estimate=LIGHT,
        name="products",
    )(where, aperture, reflection, *extra, *after)


def call(kernel, name, outs, *args, after=()):
    return pl.pallas_call(
        kernel,
        in_specs=[VMEM] * len(args) + [pl.BlockSpec(memory_space=pl.ANY)] * len(after),
        out_specs=[VMEM] * len(outs),
        out_shape=[jax.ShapeDtypeStruct(shape, BF) for shape in outs],
        compiler_params=pltpu.CompilerParams(vmem_limit_bytes=16 * MIB),
        cost_estimate=LIGHT,
        name=name,
    )(*args, *after)


def add_kernel(place, tokens, mine_ref, core_ref, *refs):
    outs = refs[tokens:]
    lanes = outs[0].shape[2]
    here = slice(place * lanes, (place + 1) * lanes)
    for index, out_ref in enumerate(outs):
        count = out_ref.shape[0]
        some = slice(index * count, (index + 1) * count)
        total = mine_ref[some, :, here].astype(jnp.float32) + core_ref[some, :, here].astype(jnp.float32)
        out_ref[...] = total.astype(BF)


def total_kernel(index, mine_ref, core_ref, far_ref, *refs):
    out_ref = refs[-1]
    count, _, lanes = out_ref.shape
    some = slice(index * count, (index + 1) * count)
    total = mine_ref[some, :, lanes:].astype(jnp.float32) + core_ref[some, :, lanes:].astype(jnp.float32)
    out_ref[...] = (total + far_ref[...].astype(jnp.float32)).astype(BF)


def pack_own_kernel(where_ref, pack_ref, mine_ref, core_ref, far_ref, *refs):
    *outer_refs, out_ref = refs
    nfreq, width, lanes = far_ref.shape
    devices, rows, _ = out_ref.shape
    rows = rows // 2
    half = where_ref[1]
    own = []
    for f in range(nfreq):
        total = mine_ref[f, :, :lanes].astype(jnp.float32) + core_ref[f, :, :lanes].astype(jnp.float32)
        own.append((total + far_ref[f].astype(jnp.float32)).astype(BF))
    outer = [ref[f] for ref in outer_refs for f in range(ref.shape[0])]
    for h, parts in ((half, own), (1 - half, outer)):
        packed = nt(pack_ref[...], jnp.concatenate(parts, axis=1)).astype(BF)
        out_ref[:, pl.ds(pl.multiple_of(h * rows, rows), rows), :] = packed.reshape(devices, rows, width)


def pack_own(where, shape, *args):
    return pl.pallas_call(
        pack_own_kernel,
        in_specs=[pl.BlockSpec(memory_space=pltpu.SMEM)] + [VMEM] * len(args),
        out_specs=VMEM,
        out_shape=jax.ShapeDtypeStruct(shape, BF),
        compiler_params=pltpu.CompilerParams(vmem_limit_bytes=16 * MIB),
        cost_estimate=LIGHT,
        name="pack_own",
    )(where, *args)


def window_kernel(dft_ref, onsets_ref, traces_ref, out_ref):
    focal, width = onsets_ref.shape
    devices, rows, _ = traces_ref.shape
    group = rows // (2 * focal)
    nfreq = dft_ref.shape[1] // 2
    step = lax.broadcasted_iota(jnp.int32, (nfreq, width), 0)
    traces = traces_ref[...].astype(jnp.float32).reshape(2 * devices, focal, group, width)
    results = []
    for j in range(focal):
        column = traces[:, j].reshape(2 * nfreq, width).astype(BF)
        time = mm(dft_ref[0], column) + mm(dft_ref[1], column)
        keep = step < onsets_ref[j : j + 1, :]
        keep = jnp.concatenate([keep, keep], axis=0)
        high, low = split(jnp.where(keep, time, 0.0))
        back = mm(dft_ref[2], high) + mm(dft_ref[2], low) + mm(dft_ref[3], high)
        results.append(back.reshape(2 * devices, group, width))
    out_ref[...] = jnp.stack(results, axis=1).reshape(out_ref.shape).astype(BF)


def final_kernel(initial_ref, update_ref, out_ref, wide_ref, block_ref, sems):
    planes, nfreq, focal, _ = initial_ref.shape
    spread(wide_ref, update_ref)
    copies = []
    for freq in range(nfreq):
        for plane in range(planes):
            value = initial_ref[plane, freq].astype(jnp.float32)
            value = value + every(wide_ref, planes * freq + plane, focal, planes * nfreq)
            block_ref[plane, freq] = value.astype(BF)
            copy = pltpu.make_async_copy(
                block_ref.at[plane, freq], out_ref.at[plane, freq], sems.at[plane, freq]
            )
            copy.start()
            copies.append(copy)
    for copy in copies:
        copy.wait()


def finish(initial, update):
    planes, nfreq, focal, sources = initial.shape
    return pl.pallas_call(
        final_kernel,
        in_specs=[VMEM, VMEM],
        out_specs=pl.BlockSpec(memory_space=pl.ANY),
        scratch_shapes=[
            wide(update),
            pltpu.VMEM(initial.shape, BF),
            pltpu.SemaphoreType.DMA((planes, nfreq)),
        ],
        out_shape=jax.ShapeDtypeStruct(initial.shape, BF),
        compiler_params=pltpu.CompilerParams(vmem_limit_bytes=16 * MIB),
        name="finish",
    )(initial, update)


def swap(values, bit):
    return lax.ppermute(values, "src", [(i, i ^ bit) for i in range(lax.axis_size("src"))])


def outward(values, columns, rows):
    pairs = []
    for x in range(columns):
        for h in range(2):
            for y in range(rows):
                for s in range(4):
                    here = ((x * 2 + h) * rows + y) * 4 + s
                    there = ((x * 2 + 1 - h) * rows + y) * 4 + (s ^ 2)
                    pairs.append((here, there))
    return lax.ppermute(values, ("freq", "src"), pairs)


def local(reflection, aperture, initial, onsets):
    planes, freq_local, receivers, sources = reflection.shape
    devices = lax.axis_size("freq")
    focal = initial.shape[2]
    focal_block = focal // devices
    columns = rows = math.isqrt(devices // 2)
    pack, to_time, to_freq = tables(columns, rows, freq_local, focal_block)
    pack = jnp.asarray(pack, BF)
    dft = jnp.asarray(np.concatenate([pair(to_time), pair(to_freq)]))
    half = (lax.axis_index("freq") // rows) % 2
    where = jnp.stack([lax.axis_index("src"), half]).astype(jnp.int32)
    plane_groups = [
        [(x * 2 + h) * rows + y for x in range(columns) for y in range(rows)] for h in range(2)
    ]
    block_rows = focal_block * freq_local * planes
    part = (freq_local, sources, focal)
    cut = (freq_local // CUTS, sources, focal)

    update = None
    for iteration in range(ITERS):
        polarity = 1.0 if iteration % 2 == 0 else -1.0

        def respond(rels, **more):
            return products(polarity, rels, rows * focal_block, where, aperture.T, reflection, initial, **more)

        send_near, send_far, left, right = respond((1, 3), update=update)
        core_near, core_far = swap(send_near, 1), swap(send_far, 1)
        (near,) = respond((0,), built=(left, right))
        totals = call(functools.partial(add_kernel, 1, 0), "add", [cut] * CUTS, near, core_near)
        far_other = [swap(total, 2) for total in totals]
        (remote,) = respond((2,), built=(left, right), after=totals)
        (total,) = call(functools.partial(add_kernel, 0, 1), "add", [part], remote, core_far, after=far_other[:1])
        far_own = swap(total, 2)
        outer = []
        for index, far in enumerate(far_other):
            (other,) = call(
                functools.partial(total_kernel, index), "total", [cut], remote, core_far, far, after=(total,)
            )
            outer.append(outward(other, columns, rows))
        shape = (devices // 2, 2 * block_rows, sources)
        responses = pack_own(where, shape, pack, near, core_near, far_own, *outer)
        traces = lax.all_to_all(responses, "freq", 0, 0, tiled=True, axis_index_groups=plane_groups)
        (truncated,) = call(
            window_kernel, "window", [(devices, block_rows, sources)], dft, onsets, traces
        )
        update = lax.all_to_all(truncated, "freq", 0, 0, tiled=True)
        update = update.reshape(devices * block_rows, sources)
    return finish(initial, update)


def solution(mesh):
    placed = (
        P(None, "freq", None, "src"),
        P(None, "src"),
        P(None, "freq", None, "src"),
        P("freq", "src"),
    )
    return jax.shard_map(
        local, mesh=mesh, in_specs=placed, out_specs=P(None, "freq", None, "src"), check_vma=False
    )
```

```python
import functools
import math

import jax
import jax.numpy as jnp
import numpy as np
from jax import lax
from jax.experimental import pallas as pl
from jax.experimental.pallas import tpu as pltpu
from jax.sharding import PartitionSpec as P

ITERS = 2
AHEAD = 4
TOGETHER = 2
CUTS = 2
TILE = 16
LANES = 128
MIB = 1024 * 1024
NT = (((1,), (1,)), ((), ()))
VMEM = pl.BlockSpec(memory_space=pltpu.VMEM)
BF = jnp.bfloat16
STAGES = (((1, 3), 38), ((0,), 36), ((2,), 32))
LIGHT = pl.CostEstimate(flops=1, bytes_accessed=1, transcendentals=0)


def mm(left, right):
    return jnp.dot(left, right, preferred_element_type=jnp.float32)


def nt(left, right):
    return lax.dot_general(left, right, NT, preferred_element_type=jnp.float32)


def split(values):
    high = values.astype(BF)
    low = (values - high.astype(values.dtype)).astype(BF)
    return high, low


def tables(columns, rows, freq_local, focal_block):
    plane_devices = columns * rows
    half = plane_devices * focal_block
    nfreq = 2 * plane_devices * freq_local
    packed = half * freq_local * 2
    pack = np.zeros((packed, packed), np.float32)
    for xy in range(plane_devices):
        for j in range(focal_block):
            for f in range(freq_local):
                for c in range(2):
                    row = ((xy * focal_block + j) * freq_local + f) * 2 + c
                    pack[row, ((f * 2 + c) * plane_devices + xy) * focal_block + j] = 1
    positions = np.arange(nfreq)
    phase = (np.outer(positions, positions) % nfreq) * (2.0 * math.pi / nfreq)
    cosine, sine = np.cos(phase), np.sin(phase)
    to_time = np.zeros((2, nfreq, nfreq, 2))
    to_time[0, :, :, 0] = cosine / nfreq
    to_time[0, :, :, 1] = -sine / nfreq
    to_time[1, :, :, 0] = sine / nfreq
    to_time[1, :, :, 1] = cosine / nfreq
    to_freq = np.zeros((nfreq, 2, 2, nfreq))
    to_freq[:, 0, 0, :] = cosine
    to_freq[:, 0, 1, :] = sine
    to_freq[:, 1, 0, :] = -sine
    to_freq[:, 1, 1, :] = cosine
    to_time = to_time.reshape(2 * nfreq, columns, 2, rows, freq_local * 2).transpose(0, 1, 3, 2, 4)
    to_time = to_time.reshape(2 * nfreq, 2 * nfreq).astype(np.float32)
    to_freq = to_freq.reshape(2 * nfreq, 2 * nfreq).astype(np.float32)
    return pack, to_time, to_freq


def pair(matrix):
    high = matrix.astype(BF)
    low = (matrix - high.astype(np.float32)).astype(BF)
    return np.stack([high, low])


def spread(wide_ref, update_ref):
    for slab in range(wide_ref.shape[0]):
        wide_ref[slab] = update_ref[:, slab * LANES : (slab + 1) * LANES].astype(jnp.float32)


def every(wide_ref, start, count, stride):
    slabs = [wide_ref[slab, pl.ds(start, count, stride), :] for slab in range(wide_ref.shape[0])]
    return jnp.concatenate(slabs, axis=1)


def wide(update):
    rows, width = update.shape
    return pltpu.VMEM((width // LANES, rows, LANES), jnp.float32)


def weights(polarity, half, block, initial_ref, update_ref, wide_ref, left_ref, right_ref):
    _, nfreq, focal, width = initial_ref.shape
    if update_ref is not None:
        spread(wide_ref, update_ref)
    for freq in range(nfreq):
        planes = []
        for plane in range(2):
            value = initial_ref[plane, freq].astype(jnp.float32)
            if update_ref is not None:
                value = value + every(wide_ref, 2 * freq + plane, focal, 2 * nfreq)
                value = value.astype(BF).astype(jnp.float32)
            value = value.reshape(focal // (2 * block), 2, block, width)
            planes.append([value[:, h].reshape(focal // 2, width) for h in range(2)])
        for place in range(2):
            real, imag = [jnp.where(half == place, low, high) for low, high in planes]
            here = slice(place * focal, (place + 1) * focal)
            left_ref[freq, :, here] = jnp.concatenate([real, imag], axis=0).T.astype(BF)
            right = jnp.concatenate([-polarity * imag, polarity * real], axis=0)
            right_ref[freq, :, here] = right.T.astype(BF)


def product_kernel(polarity, rels, build, tokens, focal_rows, where_ref, aperture_ref, reflection_ref, *refs):
    if build:
        source_ref, *refs = refs
    else:
        left_ref, right_ref, *refs = refs
    refs = refs[tokens:]
    outs, refs = refs[: len(rels)], refs[len(rels) :]
    held_ref, *refs = refs
    if build:
        left_ref, right_ref, *refs = refs
    sems, *refs = refs
    if build:
        initial_ref, initial_sem = refs
    nfreq, width, _ = outs[0].shape
    pieces = [(place, freq) for place in range(len(rels)) for freq in range(nfreq)]
    blocks = [jnp.bitwise_xor(where_ref[0], rel) for rel in rels]

    def fetch(piece, plane):
        place, freq = pieces[piece]
        return pltpu.make_async_copy(
            reflection_ref.at[plane, freq, pl.ds(blocks[place] * width, width), :],
            held_ref.at[piece, plane],
            sems.at[piece, plane],
        )

    def begin(piece):
        if piece < len(pieces):
            for plane in range(2):
                fetch(piece, plane).start()

    if build:
        load = pltpu.make_async_copy(source_ref, initial_ref, initial_sem)
        load.start()
    for piece in range(AHEAD):
        begin(piece)
    if build:
        load.wait()
        weights(polarity, where_ref[1], focal_rows, initial_ref, None, None, left_ref, right_ref)

    source_blocks, receiver_blocks = aperture_ref.shape
    strips = receiver_blocks // 4
    tall = width // strips
    wide_block = width // source_blocks

    def mask_of(place, strip):
        row = blocks[place] * strips + strip
        parts = [
            jnp.full((TILE, wide_block), aperture_ref[column, row].astype(jnp.float32)) for column in range(source_blocks)
        ]
        return jnp.concatenate(parts, axis=1).astype(BF)

    for low in range(0, len(pieces), TOGETHER):
        both = range(low, min(low + TOGETHER, len(pieces)))
        for piece in both:
            for plane in range(2):
                fetch(piece, plane).wait()
        for piece in both:
            begin(piece + AHEAD)
        for piece in both:
            place, freq = pieces[piece]
            masks = [mask_of(place, strip) for strip in range(strips)]
            masked = []
            for plane in range(2):
                parts = []
                for strip in range(strips):
                    part = held_ref[piece, plane, strip * tall : (strip + 1) * tall, :]
                    part = part.reshape(tall // TILE, TILE, width) * masks[strip][None]
                    parts.append(part.reshape(tall, width))
                masked.append(jnp.concatenate(parts, axis=0))
                held_ref[piece, plane] = masked[plane]
            total = mm(masked[0], left_ref[freq]) + mm(masked[1], right_ref[freq])
            outs[place][freq] = total.astype(BF)


def products(polarity, rels, focal_rows, limit, where, aperture, reflection, initial, built=None, after=()):
    planes, nfreq, receivers, sources = reflection.shape
    focal = initial.shape[2]
    out = jax.ShapeDtypeStruct((nfreq, sources, 2 * focal), BF)
    pieces = len(rels) * nfreq
    outs = [out] * len(rels) + [jax.ShapeDtypeStruct((pieces, planes, sources, sources), BF)]
    scratch = [pltpu.SemaphoreType.DMA((pieces, planes))]
    anywhere = pl.BlockSpec(memory_space=pl.ANY)
    smem = pl.BlockSpec(memory_space=pltpu.SMEM)
    build = built is None
    if build:
        outs += [out] * 2
        scratch += [pltpu.VMEM(initial.shape, BF), pltpu.SemaphoreType.DMA(())]
        extra, specs = [initial], [anywhere]
    else:
        extra, specs = list(built), [VMEM] * 2
    return pl.pallas_call(
        functools.partial(product_kernel, polarity, rels, build, len(after), focal_rows),
        in_specs=[smem, smem, anywhere] + specs + [anywhere] * len(after),
        out_specs=[VMEM] * len(outs),
        scratch_shapes=scratch,
        out_shape=outs,
        compiler_params=pltpu.CompilerParams(vmem_limit_bytes=limit * MIB),
        cost_estimate=LIGHT,
        name="products",
    )(where, aperture, reflection, *extra, *after)


def product_again_kernel(polarity, build, tokens, focal_rows, where_ref, held_ref, *refs):
    if build:
        initial_ref, update_ref, *refs = refs
        refs = refs[tokens:]
        *outs, left_ref, right_ref, wide_ref = refs
        weights(polarity, where_ref[1], focal_rows, initial_ref, update_ref, wide_ref, left_ref, right_ref)
    else:
        left_ref, right_ref, *refs = refs
        outs = refs[tokens:]
    nfreq = left_ref.shape[0]
    for piece in range(held_ref.shape[0]):
        freq = piece % nfreq
        total = mm(held_ref[piece, 0], left_ref[freq]) + mm(held_ref[piece, 1], right_ref[freq])
        outs[piece // nfreq][freq] = total.astype(BF)


def products_again(polarity, focal_rows, where, held, initial, update=None, built=None, after=()):
    _, nfreq, focal, sources = initial.shape
    build = built is None
    out = jax.ShapeDtypeStruct((nfreq, sources, 2 * focal), BF)
    extra = [initial, update] if build else list(built)
    outs = [out] * (held.shape[0] // nfreq + (2 if build else 0))
    return pl.pallas_call(
        functools.partial(product_again_kernel, polarity, build, len(after), focal_rows),
        in_specs=[pl.BlockSpec(memory_space=pltpu.SMEM)]
        + [VMEM] * (1 + len(extra))
        + [pl.BlockSpec(memory_space=pl.ANY)] * len(after),
        out_specs=[VMEM] * len(outs),
        scratch_shapes=[wide(update)] if build else [],
        out_shape=outs,
        compiler_params=pltpu.CompilerParams(vmem_limit_bytes=16 * MIB),
        cost_estimate=LIGHT,
        name="products_again",
    )(where, held, *extra, *after)


def call(kernel, name, outs, *args, after=()):
    return pl.pallas_call(
        kernel,
        in_specs=[VMEM] * len(args) + [pl.BlockSpec(memory_space=pl.ANY)] * len(after),
        out_specs=[VMEM] * len(outs),
        out_shape=[jax.ShapeDtypeStruct(shape, BF) for shape in outs],
        compiler_params=pltpu.CompilerParams(vmem_limit_bytes=16 * MIB),
        cost_estimate=LIGHT,
        name=name,
    )(*args, *after)


def add_kernel(place, tokens, mine_ref, core_ref, *refs):
    outs = refs[tokens:]
    lanes = outs[0].shape[2]
    here = slice(place * lanes, (place + 1) * lanes)
    for index, out_ref in enumerate(outs):
        count = out_ref.shape[0]
        some = slice(index * count, (index + 1) * count)
        total = mine_ref[some, :, here].astype(jnp.float32) + core_ref[some, :, here].astype(jnp.float32)
        out_ref[...] = total.astype(BF)


def total_kernel(index, mine_ref, core_ref, far_ref, *refs):
    out_ref = refs[-1]
    count, _, lanes = out_ref.shape
    some = slice(index * count, (index + 1) * count)
    total = mine_ref[some, :, lanes:].astype(jnp.float32) + core_ref[some, :, lanes:].astype(jnp.float32)
    out_ref[...] = (total + far_ref[...].astype(jnp.float32)).astype(BF)


def pack_own_kernel(where_ref, pack_ref, mine_ref, core_ref, far_ref, *refs):
    *outer_refs, out_ref = refs
    nfreq, width, lanes = far_ref.shape
    devices, rows, _ = out_ref.shape
    rows = rows // 2
    half = where_ref[1]
    own = []
    for f in range(nfreq):
        total = mine_ref[f, :, :lanes].astype(jnp.float32) + core_ref[f, :, :lanes].astype(jnp.float32)
        own.append((total + far_ref[f].astype(jnp.float32)).astype(BF))
    outer = [ref[f] for ref in outer_refs for f in range(ref.shape[0])]
    for h, parts in ((half, own), (1 - half, outer)):
        packed = nt(pack_ref[...], jnp.concatenate(parts, axis=1)).astype(BF)
        out_ref[:, pl.ds(pl.multiple_of(h * rows, rows), rows), :] = packed.reshape(devices, rows, width)


def pack_own(where, shape, *args):
    return pl.pallas_call(
        pack_own_kernel,
        in_specs=[pl.BlockSpec(memory_space=pltpu.SMEM)] + [VMEM] * len(args),
        out_specs=VMEM,
        out_shape=jax.ShapeDtypeStruct(shape, BF),
        compiler_params=pltpu.CompilerParams(vmem_limit_bytes=16 * MIB),
        cost_estimate=LIGHT,
        name="pack_own",
    )(where, *args)


def window_kernel(dft_ref, onsets_ref, traces_ref, out_ref):
    focal, width = onsets_ref.shape
    devices, rows, _ = traces_ref.shape
    group = rows // (2 * focal)
    nfreq = dft_ref.shape[1] // 2
    step = lax.broadcasted_iota(jnp.int32, (nfreq, width), 0)
    traces = traces_ref[...].astype(jnp.float32).reshape(2 * devices, focal, group, width)
    results = []
    for j in range(focal):
        column = traces[:, j].reshape(2 * nfreq, width).astype(BF)
        time = mm(dft_ref[0], column) + mm(dft_ref[1], column)
        keep = step < onsets_ref[j : j + 1, :]
        keep = jnp.concatenate([keep, keep], axis=0)
        high, low = split(jnp.where(keep, time, 0.0))
        back = mm(dft_ref[2], high) + mm(dft_ref[2], low) + mm(dft_ref[3], high)
        results.append(back.reshape(2 * devices, group, width))
    out_ref[...] = jnp.stack(results, axis=1).reshape(out_ref.shape).astype(BF)


def final_kernel(initial_ref, update_ref, out_ref, wide_ref, block_ref, sems):
    planes, nfreq, focal, _ = initial_ref.shape
    spread(wide_ref, update_ref)
    copies = []
    for freq in range(nfreq):
        for plane in range(planes):
            value = initial_ref[plane, freq].astype(jnp.float32)
            value = value + every(wide_ref, planes * freq + plane, focal, planes * nfreq)
            block_ref[plane, freq] = value.astype(BF)
            copy = pltpu.make_async_copy(
                block_ref.at[plane, freq], out_ref.at[plane, freq], sems.at[plane, freq]
            )
            copy.start()
            copies.append(copy)
    for copy in copies:
        copy.wait()


def finish(initial, update):
    planes, nfreq, focal, sources = initial.shape
    return pl.pallas_call(
        final_kernel,
        in_specs=[VMEM, VMEM],
        out_specs=pl.BlockSpec(memory_space=pl.ANY),
        scratch_shapes=[
            wide(update),
            pltpu.VMEM(initial.shape, BF),
            pltpu.SemaphoreType.DMA((planes, nfreq)),
        ],
        out_shape=jax.ShapeDtypeStruct(initial.shape, BF),
        compiler_params=pltpu.CompilerParams(vmem_limit_bytes=16 * MIB),
        name="finish",
    )(initial, update)


def swap(values, bit):
    return lax.ppermute(values, "src", [(i, i ^ bit) for i in range(lax.axis_size("src"))])


def outward(values, columns, rows):
    pairs = []
    for x in range(columns):
        for h in range(2):
            for y in range(rows):
                for s in range(4):
                    here = ((x * 2 + h) * rows + y) * 4 + s
                    there = ((x * 2 + 1 - h) * rows + y) * 4 + (s ^ 2)
                    pairs.append((here, there))
    return lax.ppermute(values, ("freq", "src"), pairs)


def local(reflection, aperture, initial, onsets):
    planes, freq_local, receivers, sources = reflection.shape
    devices = lax.axis_size("freq")
    focal = initial.shape[2]
    focal_block = focal // devices
    columns = rows = math.isqrt(devices // 2)
    pack, to_time, to_freq = tables(columns, rows, freq_local, focal_block)
    pack = jnp.asarray(pack, BF)
    dft = jnp.asarray(np.concatenate([pair(to_time), pair(to_freq)]))
    half = (lax.axis_index("freq") // rows) % 2
    where = jnp.stack([lax.axis_index("src"), half]).astype(jnp.int32)
    plane_groups = [
        [(x * 2 + h) * rows + y for x in range(columns) for y in range(rows)] for h in range(2)
    ]
    block_rows = focal_block * freq_local * planes
    part = (freq_local, sources, focal)
    cut = (freq_local // CUTS, sources, focal)

    focal_rows = rows * focal_block
    held = []
    update = None
    for iteration in range(ITERS):
        polarity = 1.0 if iteration % 2 == 0 else -1.0

        def respond(stage, **more):
            if iteration:
                return products_again(polarity, focal_rows, where, held[stage], initial, **more)
            rels, limit = STAGES[stage]
            results = list(products(polarity, rels, focal_rows, limit, where, aperture.T, reflection, initial, **more))
            held.append(results.pop(len(rels)))
            return results

        first = {"update": update} if iteration else {}
        send_near, send_far, left, right = respond(0, **first)
        core_near, core_far = swap(send_near, 1), swap(send_far, 1)
        (near,) = respond(1, built=(left, right))
        totals = call(functools.partial(add_kernel, 1, 0), "add", [cut] * CUTS, near, core_near)
        far_other = [swap(total, 2) for total in totals]
        (remote,) = respond(2, built=(left, right), after=totals)
        (total,) = call(functools.partial(add_kernel, 0, 1), "add", [part], remote, core_far, after=far_other[:1])
        far_own = swap(total, 2)
        outer = []
        for index, far in enumerate(far_other):
            (other,) = call(
                functools.partial(total_kernel, index), "total", [cut], remote, core_far, far, after=(total,)
            )
            outer.append(outward(other, columns, rows))
        shape = (devices // 2, 2 * block_rows, sources)
        responses = pack_own(where, shape, pack, near, core_near, far_own, *outer)
        traces = lax.all_to_all(responses, "freq", 0, 0, tiled=True, axis_index_groups=plane_groups)
        (truncated,) = call(
            window_kernel, "window", [(devices, block_rows, sources)], dft, onsets, traces
        )
        update = lax.all_to_all(truncated, "freq", 0, 0, tiled=True)
        update = update.reshape(devices * block_rows, sources)
    return finish(initial, update)


def solution(mesh):
    placed = (
        P(None, "freq", None, "src"),
        P(None, "src"),
        P(None, "freq", None, "src"),
        P("freq", "src"),
    )
    return jax.shard_map(
        local, mesh=mesh, in_specs=placed, out_specs=P(None, "freq", None, "src"), check_vma=False
    )
```

```python
import functools
import math

import jax
import jax.numpy as jnp
import numpy as np
from jax import lax
from jax.experimental import pallas as pl
from jax.experimental.pallas import tpu as pltpu
from jax.sharding import PartitionSpec as P

ITERS = 2
AHEAD = 4
TOGETHER = 2
CUTS = 2
TILE = 16
LANES = 128
MIB = 1024 * 1024
NT = (((1,), (1,)), ((), ()))
VMEM = pl.BlockSpec(memory_space=pltpu.VMEM)
BF = jnp.bfloat16
STAGES = (((1, 3), 38), ((0,), 36), ((2,), 32))
LIGHT = pl.CostEstimate(flops=1, bytes_accessed=1, transcendentals=0)


def mm(left, right):
    return jnp.dot(left, right, preferred_element_type=jnp.float32)


def nt(left, right):
    return lax.dot_general(left, right, NT, preferred_element_type=jnp.float32)


def tables(columns, rows, freq_local, focal_block):
    plane_devices = columns * rows
    half = plane_devices * focal_block
    nfreq = 2 * plane_devices * freq_local
    packed = half * freq_local * 2
    pack = np.zeros((packed, packed), np.float32)
    for xy in range(plane_devices):
        for j in range(focal_block):
            for f in range(freq_local):
                for c in range(2):
                    row = ((xy * focal_block + j) * freq_local + f) * 2 + c
                    pack[row, ((f * 2 + c) * plane_devices + xy) * focal_block + j] = 1
    positions = np.arange(nfreq)
    phase = (np.outer(positions, positions) % nfreq) * (2.0 * math.pi / nfreq)
    cosine, sine = np.cos(phase), np.sin(phase)
    to_time = np.zeros((2, nfreq, nfreq, 2))
    to_time[0, :, :, 0] = cosine / nfreq
    to_time[0, :, :, 1] = -sine / nfreq
    to_time[1, :, :, 0] = sine / nfreq
    to_time[1, :, :, 1] = cosine / nfreq
    to_freq = np.zeros((nfreq, 2, 2, nfreq))
    to_freq[:, 0, 0, :] = cosine
    to_freq[:, 0, 1, :] = sine
    to_freq[:, 1, 0, :] = -sine
    to_freq[:, 1, 1, :] = cosine
    to_time = to_time.reshape(2 * nfreq, columns, 2, rows, freq_local * 2).transpose(0, 1, 3, 2, 4)
    to_time = to_time.reshape(2 * nfreq, 2 * nfreq).astype(np.float32)
    to_freq = to_freq.reshape(2 * nfreq, 2 * nfreq).astype(np.float32)
    return pack, to_time, to_freq


def pair(matrix):
    high = matrix.astype(BF)
    low = (matrix - high.astype(np.float32)).astype(BF)
    return np.stack([high, low])


def spread(wide_ref, update_ref):
    for slab in range(wide_ref.shape[0]):
        wide_ref[slab] = update_ref[:, slab * LANES : (slab + 1) * LANES].astype(jnp.float32)


def every(wide_ref, start, count, stride):
    slabs = [wide_ref[slab, pl.ds(start, count, stride), :] for slab in range(wide_ref.shape[0])]
    return jnp.concatenate(slabs, axis=1)


def wide(update):
    rows, width = update.shape
    return pltpu.VMEM((width // LANES, rows, LANES), jnp.float32)


def weights(polarity, half, block, freqs, initial_ref, wide_ref, left_ref, right_ref):
    _, nfreq, focal, width = initial_ref.shape
    for freq in freqs:
        planes = []
        for plane in range(2):
            value = initial_ref[plane, freq].astype(jnp.float32)
            if wide_ref is not None:
                value = value + every(wide_ref, 2 * freq + plane, focal, 2 * nfreq)
                value = value.astype(BF).astype(jnp.float32)
            value = value.reshape(focal // (2 * block), 2, block, width)
            planes.append([value[:, h].reshape(focal // 2, width) for h in range(2)])
        for place in range(2):
            real, imag = [jnp.where(half == place, low, high) for low, high in planes]
            here = slice(place * focal, (place + 1) * focal)
            left_ref[freq, :, here] = jnp.concatenate([real, imag], axis=0).T.astype(BF)
            right = jnp.concatenate([-polarity * imag, polarity * real], axis=0)
            right_ref[freq, :, here] = right.T.astype(BF)


def product_kernel(polarity, rels, build, tokens, focal_rows, blocks_shape, where_ref, reflection_ref, *refs):
    if build:
        source_ref, *refs = refs
    else:
        left_ref, right_ref, *refs = refs
    refs = refs[tokens:]
    outs, refs = refs[: len(rels)], refs[len(rels) :]
    held_ref, *refs = refs
    if build:
        left_ref, right_ref, *refs = refs
    sems, *refs = refs
    if build:
        initial_ref, initial_sem = refs
    nfreq, width, _ = outs[0].shape
    pieces = [(place, freq) for place in range(len(rels)) for freq in range(nfreq)]
    blocks = [jnp.bitwise_xor(where_ref[0], rel) for rel in rels]

    def fetch(piece, plane):
        place, freq = pieces[piece]
        return pltpu.make_async_copy(
            reflection_ref.at[plane, freq, pl.ds(blocks[place] * width, width), :],
            held_ref.at[piece, plane],
            sems.at[piece, plane],
        )

    def begin(piece):
        if piece < len(pieces):
            for plane in range(2):
                fetch(piece, plane).start()

    if build:
        load = pltpu.make_async_copy(source_ref, initial_ref, initial_sem)
        load.start()
    for piece in range(AHEAD):
        begin(piece)
    if build:
        load.wait()
        weights(polarity, where_ref[1], focal_rows, range(nfreq), initial_ref, None, left_ref, right_ref)

    source_blocks, receiver_blocks = blocks_shape
    strips = receiver_blocks // 4
    tall = width // strips
    wide_block = width // source_blocks

    def mask_of(place, strip):
        row = blocks[place] * strips + strip
        within = [where_ref[2 + column * receiver_blocks + row] for column in range(source_blocks)]
        parts = [jnp.full((TILE, wide_block), value.astype(jnp.float32)) for value in within]
        return jnp.concatenate(parts, axis=1).astype(BF)

    for low in range(0, len(pieces), TOGETHER):
        both = range(low, min(low + TOGETHER, len(pieces)))
        for piece in both:
            for plane in range(2):
                fetch(piece, plane).wait()
        for piece in both:
            begin(piece + AHEAD)
        for piece in both:
            place, freq = pieces[piece]
            masks = [mask_of(place, strip) for strip in range(strips)]
            masked = []
            for plane in range(2):
                parts = []
                for strip in range(strips):
                    part = held_ref[piece, plane, strip * tall : (strip + 1) * tall, :]
                    part = part.reshape(tall // TILE, TILE, width) * masks[strip][None]
                    parts.append(part.reshape(tall, width))
                masked.append(jnp.concatenate(parts, axis=0))
                held_ref[piece, plane] = masked[plane]
            total = mm(masked[0], left_ref[freq]) + mm(masked[1], right_ref[freq])
            outs[place][freq] = total.astype(BF)


def products(polarity, rels, focal_rows, limit, blocks, where, reflection, initial, built=None, after=()):
    planes, nfreq, receivers, sources = reflection.shape
    focal = initial.shape[2]
    out = jax.ShapeDtypeStruct((nfreq, sources, 2 * focal), BF)
    pieces = len(rels) * nfreq
    outs = [out] * len(rels) + [jax.ShapeDtypeStruct((pieces, planes, sources, sources), BF)]
    scratch = [pltpu.SemaphoreType.DMA((pieces, planes))]
    anywhere = pl.BlockSpec(memory_space=pl.ANY)
    smem = pl.BlockSpec(memory_space=pltpu.SMEM)
    build = built is None
    if build:
        outs += [out] * 2
        scratch += [pltpu.VMEM(initial.shape, BF), pltpu.SemaphoreType.DMA(())]
        extra, specs = [initial], [anywhere]
    else:
        extra, specs = list(built), [VMEM] * 2
    return pl.pallas_call(
        functools.partial(product_kernel, polarity, rels, build, len(after), focal_rows, blocks),
        in_specs=[smem, anywhere] + specs + [anywhere] * len(after),
        out_specs=[VMEM] * len(outs),
        scratch_shapes=scratch,
        out_shape=outs,
        compiler_params=pltpu.CompilerParams(vmem_limit_bytes=limit * MIB),
        cost_estimate=LIGHT,
        name="products",
    )(where, reflection, *extra, *after)


def product_again_kernel(polarity, build, tokens, focal_rows, where_ref, held_ref, *refs):
    if build:
        initial_ref, update_ref, *refs = refs
        refs = refs[tokens:]
        *outs, left_ref, right_ref, wide_ref = refs
        spread(wide_ref, update_ref)
    else:
        left_ref, right_ref, *refs = refs
        outs = refs[tokens:]
    nfreq = left_ref.shape[0]
    for freq in range(nfreq):
        if build:
            weights(polarity, where_ref[1], focal_rows, (freq,), initial_ref, wide_ref, left_ref, right_ref)
        for place, out_ref in enumerate(outs):
            piece = place * nfreq + freq
            total = mm(held_ref[piece, 0], left_ref[freq]) + mm(held_ref[piece, 1], right_ref[freq])
            out_ref[freq] = total.astype(BF)


def products_again(polarity, focal_rows, where, held, initial, update=None, built=None, after=()):
    _, nfreq, focal, sources = initial.shape
    build = built is None
    out = jax.ShapeDtypeStruct((nfreq, sources, 2 * focal), BF)
    extra = [initial, update] if build else list(built)
    outs = [out] * (held.shape[0] // nfreq + (2 if build else 0))
    return pl.pallas_call(
        functools.partial(product_again_kernel, polarity, build, len(after), focal_rows),
        in_specs=[pl.BlockSpec(memory_space=pltpu.SMEM)]
        + [VMEM] * (1 + len(extra))
        + [pl.BlockSpec(memory_space=pl.ANY)] * len(after),
        out_specs=[VMEM] * len(outs),
        scratch_shapes=[wide(update)] if build else [],
        out_shape=outs,
        compiler_params=pltpu.CompilerParams(vmem_limit_bytes=16 * MIB),
        cost_estimate=LIGHT,
        name="products_again",
    )(where, held, *extra, *after)


def call(kernel, name, outs, *args, after=()):
    return pl.pallas_call(
        kernel,
        in_specs=[VMEM] * len(args) + [pl.BlockSpec(memory_space=pl.ANY)] * len(after),
        out_specs=[VMEM] * len(outs),
        out_shape=[jax.ShapeDtypeStruct(shape, BF) for shape in outs],
        compiler_params=pltpu.CompilerParams(vmem_limit_bytes=16 * MIB),
        cost_estimate=LIGHT,
        name=name,
    )(*args, *after)


def add_kernel(place, tokens, mine_ref, core_ref, *refs):
    outs = refs[tokens:]
    lanes = outs[0].shape[2]
    here = slice(place * lanes, (place + 1) * lanes)
    for index, out_ref in enumerate(outs):
        count = out_ref.shape[0]
        some = slice(index * count, (index + 1) * count)
        total = mine_ref[some, :, here].astype(jnp.float32) + core_ref[some, :, here].astype(jnp.float32)
        out_ref[...] = total.astype(BF)


def total_kernel(index, mine_ref, core_ref, far_ref, *refs):
    out_ref = refs[-1]
    count, _, lanes = out_ref.shape
    some = slice(index * count, (index + 1) * count)
    total = mine_ref[some, :, lanes:].astype(jnp.float32) + core_ref[some, :, lanes:].astype(jnp.float32)
    out_ref[...] = (total + far_ref[...].astype(jnp.float32)).astype(BF)


def pack_own_kernel(where_ref, pack_ref, mine_ref, core_ref, far_ref, *refs):
    *outer_refs, out_ref = refs
    nfreq, width, lanes = far_ref.shape
    group = 2 * nfreq
    mine = where_ref[1] == 0
    outer = [ref[f] for ref in outer_refs for f in range(ref.shape[0])]
    halves = [[], []]
    for f in range(nfreq):
        total = mine_ref[f, :, :lanes].astype(jnp.float32) + core_ref[f, :, :lanes].astype(jnp.float32)
        own = (total + far_ref[f].astype(jnp.float32)).astype(BF)
        halves[0].append(jnp.where(mine, own, outer[f]))
        halves[1].append(jnp.where(mine, outer[f], own))
    packed = [nt(pack_ref[...], jnp.concatenate(parts, axis=1)) for parts in halves]
    packed = [part.reshape(part.shape[0] // group, group, width) for part in packed]
    out_ref[...] = jnp.stack(packed, axis=1).reshape(out_ref.shape).astype(BF)


def pack_own(where, shape, *args):
    return pl.pallas_call(
        pack_own_kernel,
        in_specs=[pl.BlockSpec(memory_space=pltpu.SMEM)] + [VMEM] * len(args),
        out_specs=VMEM,
        out_shape=jax.ShapeDtypeStruct(shape, BF),
        compiler_params=pltpu.CompilerParams(vmem_limit_bytes=16 * MIB),
        cost_estimate=LIGHT,
        name="pack_own",
    )(where, *args)


def window_kernel(dft_ref, onsets_ref, traces_ref, out_ref):
    focal, width = onsets_ref.shape
    devices, rows, _ = traces_ref.shape
    rows = rows // focal
    nfreq = dft_ref.shape[1] // 2
    step = lax.broadcasted_iota(jnp.int32, (nfreq, width), 0)
    results = []
    for j in range(focal):
        column = traces_ref[:, j * rows : (j + 1) * rows, :].reshape(2 * nfreq, width)
        time = mm(dft_ref[0], column) + mm(dft_ref[1], column)
        keep = step < onsets_ref[j : j + 1, :]
        keep = jnp.concatenate([keep, keep], axis=0)
        time = jnp.where(keep, time, 0.0).astype(BF)
        back = mm(dft_ref[2], time) + mm(dft_ref[3], time)
        results.append(back.reshape(2 * devices, rows // 2, width))
    out_ref[...] = jnp.stack(results, axis=1).reshape(out_ref.shape).astype(BF)


def final_kernel(initial_ref, update_ref, out_ref, wide_ref, block_ref, sems):
    planes, nfreq, focal, _ = initial_ref.shape
    spread(wide_ref, update_ref)
    copies = []
    for freq in range(nfreq):
        for plane in range(planes):
            value = initial_ref[plane, freq].astype(jnp.float32)
            value = value + every(wide_ref, planes * freq + plane, focal, planes * nfreq)
            block_ref[plane, freq] = value.astype(BF)
            copy = pltpu.make_async_copy(
                block_ref.at[plane, freq], out_ref.at[plane, freq], sems.at[plane, freq]
            )
            copy.start()
            copies.append(copy)
    for copy in copies:
        copy.wait()


def finish(initial, update):
    planes, nfreq, focal, sources = initial.shape
    return pl.pallas_call(
        final_kernel,
        in_specs=[VMEM, VMEM],
        out_specs=pl.BlockSpec(memory_space=pl.ANY),
        scratch_shapes=[
            wide(update),
            pltpu.VMEM(initial.shape, BF),
            pltpu.SemaphoreType.DMA((planes, nfreq)),
        ],
        out_shape=jax.ShapeDtypeStruct(initial.shape, BF),
        compiler_params=pltpu.CompilerParams(vmem_limit_bytes=16 * MIB),
        name="finish",
    )(initial, update)


def swap(values, bit):
    return lax.ppermute(values, "src", [(i, i ^ bit) for i in range(lax.axis_size("src"))])


def outward(values, columns, rows):
    pairs = []
    for x in range(columns):
        for h in range(2):
            for y in range(rows):
                for s in range(4):
                    here = ((x * 2 + h) * rows + y) * 4 + s
                    there = ((x * 2 + 1 - h) * rows + y) * 4 + (s ^ 2)
                    pairs.append((here, there))
    return lax.ppermute(values, ("freq", "src"), pairs)


def local(reflection, aperture, initial, onsets):
    planes, freq_local, receivers, sources = reflection.shape
    devices = lax.axis_size("freq")
    focal = initial.shape[2]
    focal_block = focal // devices
    columns = rows = math.isqrt(devices // 2)
    pack, to_time, to_freq = tables(columns, rows, freq_local, focal_block)
    pack = jnp.asarray(pack, BF)
    dft = jnp.asarray(np.concatenate([pair(to_time), pair(to_freq)]))
    half = (lax.axis_index("freq") // rows) % 2
    where = jnp.stack([lax.axis_index("src"), half]).astype(jnp.int32)
    where = jnp.concatenate([where, aperture.T.reshape(-1)])
    blocks = aperture.shape[::-1]
    plane_groups = [
        [(x * 2 + h) * rows + y for x in range(columns) for y in range(rows)] for h in range(2)
    ]
    block_rows = focal_block * freq_local * planes
    part = (freq_local, sources, focal)
    cut = (freq_local // CUTS, sources, focal)

    focal_rows = rows * focal_block
    held = []
    update = None
    for iteration in range(ITERS):
        polarity = 1.0 if iteration % 2 == 0 else -1.0

        def respond(stage, **more):
            if iteration:
                return products_again(polarity, focal_rows, where, held[stage], initial, **more)
            rels, limit = STAGES[stage]
            results = list(products(polarity, rels, focal_rows, limit, blocks, where, reflection, initial, **more))
            held.append(results.pop(len(rels)))
            return results

        first = {"update": update} if iteration else {}
        send_near, send_far, left, right = respond(0, **first)
        core_near, core_far = swap(send_near, 1), swap(send_far, 1)
        (near,) = respond(1, built=(left, right))
        totals = call(functools.partial(add_kernel, 1, 0), "add", [cut] * CUTS, near, core_near)
        far_other = [swap(total, 2) for total in totals]
        (remote,) = respond(2, built=(left, right), after=totals)
        (total,) = call(functools.partial(add_kernel, 0, 1), "add", [part], remote, core_far, after=far_other[:1])
        far_own = swap(total, 2)
        outer = []
        for index, far in enumerate(far_other):
            (other,) = call(
                functools.partial(total_kernel, index), "total", [cut], remote, core_far, far, after=(total,)
            )
            outer.append(outward(other, columns, rows))
        shape = (devices // 2, 2 * block_rows, sources)
        responses = pack_own(where, shape, pack, near, core_near, far_own, *outer)
        traces = lax.all_to_all(responses, "freq", 0, 0, tiled=True, axis_index_groups=plane_groups)
        (truncated,) = call(
            window_kernel, "window", [(devices, block_rows, sources)], dft, onsets, traces
        )
        update = lax.all_to_all(truncated, "freq", 0, 0, tiled=True)
        update = update.reshape(devices * block_rows, sources)
    return finish(initial, update)


def solution(mesh):
    placed = (
        P(None, "freq", None, "src"),
        P(None, "src"),
        P(None, "freq", None, "src"),
        P("freq", "src"),
    )
    return jax.shard_map(
        local, mesh=mesh, in_specs=placed, out_specs=P(None, "freq", None, "src"), check_vma=False
    )
```

```python
import functools
import math

import jax
import jax.numpy as jnp
import numpy as np
from jax import lax
from jax.experimental import pallas as pl
from jax.experimental.pallas import tpu as pltpu
from jax.sharding import PartitionSpec as P

ITERS = 2
AHEAD = 4
TOGETHER = 2
CUTS = 2
TILE = 16
LANES = 128
MIB = 1024 * 1024
NT = (((1,), (1,)), ((), ()))
VMEM = pl.BlockSpec(memory_space=pltpu.VMEM)
BF = jnp.bfloat16
STAGES = (((1, 3), 38), ((0,), 36), ((2,), 32))
LIGHT = pl.CostEstimate(flops=1, bytes_accessed=1, transcendentals=0)


def mm(left, right):
    return jnp.dot(left, right, preferred_element_type=jnp.float32)


def nt(left, right):
    return lax.dot_general(left, right, NT, preferred_element_type=jnp.float32)


def tables(columns, rows, freq_local, focal_block):
    plane_devices = columns * rows
    half = plane_devices * focal_block
    nfreq = 2 * plane_devices * freq_local
    packed = half * freq_local * 2
    pack = np.zeros((packed, packed), np.float32)
    for xy in range(plane_devices):
        for j in range(focal_block):
            for f in range(freq_local):
                for c in range(2):
                    row = ((xy * focal_block + j) * freq_local + f) * 2 + c
                    pack[row, ((f * 2 + c) * plane_devices + xy) * focal_block + j] = 1
    positions = np.arange(nfreq)
    phase = (np.outer(positions, positions) % nfreq) * (2.0 * math.pi / nfreq)
    cosine, sine = np.cos(phase), np.sin(phase)
    to_time = np.zeros((2, nfreq, nfreq, 2))
    to_time[0, :, :, 0] = cosine / nfreq
    to_time[0, :, :, 1] = -sine / nfreq
    to_time[1, :, :, 0] = sine / nfreq
    to_time[1, :, :, 1] = cosine / nfreq
    to_freq = np.zeros((nfreq, 2, 2, nfreq))
    to_freq[:, 0, 0, :] = cosine
    to_freq[:, 0, 1, :] = sine
    to_freq[:, 1, 0, :] = -sine
    to_freq[:, 1, 1, :] = cosine
    to_time = to_time.reshape(2 * nfreq, columns, 2, rows, freq_local * 2).transpose(0, 1, 3, 2, 4)
    to_time = to_time.reshape(2 * nfreq, 2 * nfreq).astype(np.float32)
    to_freq = to_freq.reshape(2 * nfreq, 2 * nfreq).astype(np.float32)
    return pack, to_time, to_freq


def pair(matrix):
    high = matrix.astype(BF)
    low = (matrix - high.astype(np.float32)).astype(BF)
    return np.stack([high, low])


def spread(wide_ref, update_ref):
    for slab in range(wide_ref.shape[0]):
        wide_ref[slab] = update_ref[:, slab * LANES : (slab + 1) * LANES].astype(jnp.float32)


def every(wide_ref, start, count, stride):
    slabs = [wide_ref[slab, pl.ds(start, count, stride), :] for slab in range(wide_ref.shape[0])]
    return jnp.concatenate(slabs, axis=1)


def wide(update):
    rows, width = update.shape
    return pltpu.VMEM((width // LANES, rows, LANES), jnp.float32)


def weights(polarity, half, block, freqs, initial_ref, wide_ref, left_ref, right_ref):
    _, nfreq, focal, width = initial_ref.shape
    for freq in freqs:
        planes = []
        for plane in range(2):
            value = initial_ref[plane, freq].astype(jnp.float32)
            if wide_ref is not None:
                value = value + every(wide_ref, 2 * freq + plane, focal, 2 * nfreq)
                value = value.astype(BF).astype(jnp.float32)
            value = value.reshape(focal // (2 * block), 2, block, width)
            planes.append([value[:, h].reshape(focal // 2, width) for h in range(2)])
        for place in range(2):
            real, imag = [jnp.where(half == place, low, high) for low, high in planes]
            here = slice(place * focal, (place + 1) * focal)
            left_ref[freq, :, here] = jnp.concatenate([real, imag], axis=0).T.astype(BF)
            right = jnp.concatenate([-polarity * imag, polarity * real], axis=0)
            right_ref[freq, :, here] = right.T.astype(BF)


def product_kernel(polarity, rels, build, tokens, focal_rows, blocks_shape, where_ref, reflection_ref, *refs):
    if build:
        source_ref, *refs = refs
    else:
        left_ref, right_ref, *refs = refs
    refs = refs[tokens:]
    outs, refs = refs[: len(rels)], refs[len(rels) :]
    held_ref, *refs = refs
    if build:
        left_ref, right_ref, *refs = refs
    sems, *refs = refs
    if build:
        initial_ref, initial_sem = refs
    nfreq, width, _ = outs[0].shape
    pieces = [(place, freq) for place in range(len(rels)) for freq in range(nfreq)]
    blocks = [jnp.bitwise_xor(where_ref[0], rel) for rel in rels]

    def fetch(piece, plane):
        place, freq = pieces[piece]
        return pltpu.make_async_copy(
            reflection_ref.at[plane, freq, pl.ds(blocks[place] * width, width), :],
            held_ref.at[piece, plane],
            sems.at[piece, plane],
        )

    def begin(piece):
        if piece < len(pieces):
            for plane in range(2):
                fetch(piece, plane).start()

    if build:
        load = pltpu.make_async_copy(source_ref, initial_ref, initial_sem)
        load.start()
    for piece in range(AHEAD):
        begin(piece)
    if build:
        load.wait()
        weights(polarity, where_ref[1], focal_rows, range(nfreq), initial_ref, None, left_ref, right_ref)

    source_blocks, receiver_blocks = blocks_shape
    strips = receiver_blocks // 4
    tall = width // strips
    wide_block = width // source_blocks

    def mask_of(place, strip):
        row = blocks[place] * strips + strip
        within = [where_ref[2 + column * receiver_blocks + row] for column in range(source_blocks)]
        parts = [jnp.full((TILE, wide_block), value.astype(jnp.float32)) for value in within]
        return jnp.concatenate(parts, axis=1).astype(BF)

    for low in range(0, len(pieces), TOGETHER):
        both = range(low, min(low + TOGETHER, len(pieces)))
        for piece in both:
            for plane in range(2):
                fetch(piece, plane).wait()
        for piece in both:
            begin(piece + AHEAD)
        for piece in both:
            place, freq = pieces[piece]
            masks = [mask_of(place, strip) for strip in range(strips)]
            masked = []
            for plane in range(2):
                parts = []
                for strip in range(strips):
                    part = held_ref[piece, plane, strip * tall : (strip + 1) * tall, :]
                    part = part.reshape(tall // TILE, TILE, width) * masks[strip][None]
                    parts.append(part.reshape(tall, width))
                masked.append(jnp.concatenate(parts, axis=0))
                held_ref[piece, plane] = masked[plane]
            total = mm(masked[0], left_ref[freq]) + mm(masked[1], right_ref[freq])
            outs[place][freq] = total.astype(BF)


def products(polarity, rels, focal_rows, limit, blocks, where, reflection, initial, built=None, after=()):
    planes, nfreq, receivers, sources = reflection.shape
    focal = initial.shape[2]
    out = jax.ShapeDtypeStruct((nfreq, sources, 2 * focal), BF)
    pieces = len(rels) * nfreq
    outs = [out] * len(rels) + [jax.ShapeDtypeStruct((pieces, planes, sources, sources), BF)]
    scratch = [pltpu.SemaphoreType.DMA((pieces, planes))]
    anywhere = pl.BlockSpec(memory_space=pl.ANY)
    smem = pl.BlockSpec(memory_space=pltpu.SMEM)
    build = built is None
    if build:
        outs += [out] * 2
        scratch += [pltpu.VMEM(initial.shape, BF), pltpu.SemaphoreType.DMA(())]
        extra, specs = [initial], [anywhere]
    else:
        extra, specs = list(built), [VMEM] * 2
    return pl.pallas_call(
        functools.partial(product_kernel, polarity, rels, build, len(after), focal_rows, blocks),
        in_specs=[smem, anywhere] + specs + [anywhere] * len(after),
        out_specs=[VMEM] * len(outs),
        scratch_shapes=scratch,
        out_shape=outs,
        compiler_params=pltpu.CompilerParams(vmem_limit_bytes=limit * MIB),
        cost_estimate=LIGHT,
        name="products",
    )(where, reflection, *extra, *after)


def product_again_kernel(polarity, build, tokens, focal_rows, where_ref, held_ref, *refs):
    if build:
        initial_ref, update_ref, *refs = refs
        refs = refs[tokens:]
        *outs, left_ref, right_ref, wide_ref = refs
        spread(wide_ref, update_ref)
    else:
        left_ref, right_ref, *refs = refs
        outs = refs[tokens:]
    nfreq = left_ref.shape[0]
    for freq in range(nfreq):
        if build:
            weights(polarity, where_ref[1], focal_rows, (freq,), initial_ref, wide_ref, left_ref, right_ref)
        for place, out_ref in enumerate(outs):
            piece = place * nfreq + freq
            total = mm(held_ref[piece, 0], left_ref[freq]) + mm(held_ref[piece, 1], right_ref[freq])
            out_ref[freq] = total.astype(BF)


def products_again(polarity, focal_rows, where, held, initial, update=None, built=None, after=()):
    _, nfreq, focal, sources = initial.shape
    build = built is None
    out = jax.ShapeDtypeStruct((nfreq, sources, 2 * focal), BF)
    extra = [initial, update] if build else list(built)
    outs = [out] * (held.shape[0] // nfreq + (2 if build else 0))
    return pl.pallas_call(
        functools.partial(product_again_kernel, polarity, build, len(after), focal_rows),
        in_specs=[pl.BlockSpec(memory_space=pltpu.SMEM)]
        + [VMEM] * (1 + len(extra))
        + [pl.BlockSpec(memory_space=pl.ANY)] * len(after),
        out_specs=[VMEM] * len(outs),
        scratch_shapes=[wide(update)] if build else [],
        out_shape=outs,
        compiler_params=pltpu.CompilerParams(vmem_limit_bytes=16 * MIB),
        cost_estimate=LIGHT,
        name="products_again",
    )(where, held, *extra, *after)


def call(kernel, name, outs, *args, after=()):
    return pl.pallas_call(
        kernel,
        in_specs=[VMEM] * len(args) + [pl.BlockSpec(memory_space=pl.ANY)] * len(after),
        out_specs=[VMEM] * len(outs),
        out_shape=[jax.ShapeDtypeStruct(shape, BF) for shape in outs],
        compiler_params=pltpu.CompilerParams(vmem_limit_bytes=16 * MIB),
        cost_estimate=LIGHT,
        name=name,
    )(*args, *after)


def add_kernel(place, tokens, mine_ref, core_ref, *refs):
    outs = refs[tokens:]
    lanes = outs[0].shape[2]
    here = slice(place * lanes, (place + 1) * lanes)
    low = 0
    for out_ref in outs:
        some = slice(low, low + out_ref.shape[1])
        low += out_ref.shape[1]
        total = mine_ref[:, some, here].astype(jnp.float32) + core_ref[:, some, here].astype(jnp.float32)
        out_ref[...] = total.astype(BF)


def total_kernel(index, pack_ref, mine_ref, core_ref, far_ref, *refs):
    out_ref = refs[-1]
    nfreq, count, lanes = far_ref.shape
    some = slice(index * count, (index + 1) * count)
    parts = []
    for f in range(nfreq):
        total = mine_ref[f, some, lanes:].astype(jnp.float32) + core_ref[f, some, lanes:].astype(jnp.float32)
        parts.append((total + far_ref[f].astype(jnp.float32)).astype(BF))
    packed = nt(pack_ref[...], jnp.concatenate(parts, axis=1))
    out_ref[...] = packed.reshape(out_ref.shape).astype(BF)


def pack_own_kernel(where_ref, pack_ref, mine_ref, core_ref, far_ref, *refs):
    *outer_refs, out_ref = refs
    nfreq, width, lanes = far_ref.shape
    group = 2 * nfreq
    mine = where_ref[1] == 0
    parts = []
    for f in range(nfreq):
        total = mine_ref[f, :, :lanes].astype(jnp.float32) + core_ref[f, :, :lanes].astype(jnp.float32)
        parts.append((total + far_ref[f].astype(jnp.float32)).astype(BF))
    own = nt(pack_ref[...], jnp.concatenate(parts, axis=1))
    outer = [ref[...].astype(jnp.float32).reshape(own.shape[0], ref.shape[2]) for ref in outer_refs]
    outer = jnp.concatenate(outer, axis=1)
    packed = [jnp.where(mine, own, outer), jnp.where(mine, outer, own)]
    packed = [part.reshape(part.shape[0] // group, group, width) for part in packed]
    out_ref[...] = jnp.stack(packed, axis=1).reshape(out_ref.shape).astype(BF)


def pack_own(where, shape, *args):
    return pl.pallas_call(
        pack_own_kernel,
        in_specs=[pl.BlockSpec(memory_space=pltpu.SMEM)] + [VMEM] * len(args),
        out_specs=VMEM,
        out_shape=jax.ShapeDtypeStruct(shape, BF),
        compiler_params=pltpu.CompilerParams(vmem_limit_bytes=16 * MIB),
        cost_estimate=LIGHT,
        name="pack_own",
    )(where, *args)


def window_kernel(dft_ref, onsets_ref, traces_ref, out_ref):
    focal, width = onsets_ref.shape
    devices, rows, _ = traces_ref.shape
    rows = rows // focal
    nfreq = dft_ref.shape[1] // 2
    step = lax.broadcasted_iota(jnp.int32, (nfreq, width), 0)
    size = dft_ref.shape[1]
    to_time = dft_ref[0:2].reshape(2 * size, size)
    to_freq = dft_ref[2:4].reshape(2 * size, size)

    def twice(parts, values):
        both = mm(parts, values)
        return both[:size] + both[size:]

    results = []
    for j in range(focal):
        column = traces_ref[:, j * rows : (j + 1) * rows, :].reshape(2 * nfreq, width)
        time = twice(to_time, column)
        keep = step < onsets_ref[j : j + 1, :]
        keep = jnp.concatenate([keep, keep], axis=0)
        time = jnp.where(keep, time, 0.0).astype(BF)
        back = twice(to_freq, time)
        results.append(back.reshape(2 * devices, rows // 2, width))
    out_ref[...] = jnp.stack(results, axis=1).reshape(out_ref.shape).astype(BF)


def final_kernel(initial_ref, update_ref, out_ref, wide_ref, block_ref, sems):
    planes, nfreq, focal, _ = initial_ref.shape
    spread(wide_ref, update_ref)
    copies = []
    for freq in range(nfreq):
        for plane in range(planes):
            value = initial_ref[plane, freq].astype(jnp.float32)
            value = value + every(wide_ref, planes * freq + plane, focal, planes * nfreq)
            block_ref[plane, freq] = value.astype(BF)
            copy = pltpu.make_async_copy(
                block_ref.at[plane, freq], out_ref.at[plane, freq], sems.at[plane, freq]
            )
            copy.start()
            copies.append(copy)
    for copy in copies:
        copy.wait()


def finish(initial, update):
    planes, nfreq, focal, sources = initial.shape
    return pl.pallas_call(
        final_kernel,
        in_specs=[VMEM, VMEM],
        out_specs=pl.BlockSpec(memory_space=pl.ANY),
        scratch_shapes=[
            wide(update),
            pltpu.VMEM(initial.shape, BF),
            pltpu.SemaphoreType.DMA((planes, nfreq)),
        ],
        out_shape=jax.ShapeDtypeStruct(initial.shape, BF),
        compiler_params=pltpu.CompilerParams(vmem_limit_bytes=16 * MIB),
        name="finish",
    )(initial, update)


def swap(values, bit):
    return lax.ppermute(values, "src", [(i, i ^ bit) for i in range(lax.axis_size("src"))])


def outward(values, columns, rows):
    pairs = []
    for x in range(columns):
        for h in range(2):
            for y in range(rows):
                for s in range(4):
                    here = ((x * 2 + h) * rows + y) * 4 + s
                    there = ((x * 2 + 1 - h) * rows + y) * 4 + (s ^ 2)
                    pairs.append((here, there))
    return lax.ppermute(values, ("freq", "src"), pairs)


def local(reflection, aperture, initial, onsets):
    planes, freq_local, receivers, sources = reflection.shape
    devices = lax.axis_size("freq")
    focal = initial.shape[2]
    focal_block = focal // devices
    columns = rows = math.isqrt(devices // 2)
    pack, to_time, to_freq = tables(columns, rows, freq_local, focal_block)
    pack = jnp.asarray(pack, BF)
    dft = jnp.asarray(np.concatenate([pair(to_time), pair(to_freq)]))
    half = (lax.axis_index("freq") // rows) % 2
    where = jnp.stack([lax.axis_index("src"), half]).astype(jnp.int32)
    where = jnp.concatenate([where, aperture.T.reshape(-1)])
    blocks = aperture.shape[::-1]
    plane_groups = [
        [(x * 2 + h) * rows + y for x in range(columns) for y in range(rows)] for h in range(2)
    ]
    block_rows = focal_block * freq_local * planes
    part = (freq_local, sources, focal)
    cut = (freq_local, sources // CUTS, focal)
    packed_cut = (devices // 2, block_rows, sources // CUTS)

    focal_rows = rows * focal_block
    held = []
    update = None
    for iteration in range(ITERS):
        polarity = 1.0 if iteration % 2 == 0 else -1.0

        def respond(stage, **more):
            if iteration:
                return products_again(polarity, focal_rows, where, held[stage], initial, **more)
            rels, limit = STAGES[stage]
            results = list(products(polarity, rels, focal_rows, limit, blocks, where, reflection, initial, **more))
            held.append(results.pop(len(rels)))
            return results

        first = {"update": update} if iteration else {}
        send_near, send_far, left, right = respond(0, **first)
        core_near, core_far = swap(send_near, 1), swap(send_far, 1)
        (near,) = respond(1, built=(left, right))
        totals = call(functools.partial(add_kernel, 1, 0), "add", [cut] * CUTS, near, core_near)
        far_other = [swap(total, 2) for total in totals]
        (remote,) = respond(2, built=(left, right), after=totals)
        (total,) = call(functools.partial(add_kernel, 0, 1), "add", [part], remote, core_far, after=far_other[:1])
        far_own = swap(total, 2)
        outer = []
        for index, far in enumerate(far_other):
            (other,) = call(
                functools.partial(total_kernel, index), "total", [packed_cut], pack, remote, core_far, far, after=(total,)
            )
            outer.append(outward(other, columns, rows))
        shape = (devices // 2, 2 * block_rows, sources)
        responses = pack_own(where, shape, pack, near, core_near, far_own, *outer)
        traces = lax.all_to_all(responses, "freq", 0, 0, tiled=True, axis_index_groups=plane_groups)
        (truncated,) = call(
            window_kernel, "window", [(devices, block_rows, sources)], dft, onsets, traces
        )
        update = lax.all_to_all(truncated, "freq", 0, 0, tiled=True)
        update = update.reshape(devices * block_rows, sources)
    return finish(initial, update)


def solution(mesh):
    placed = (
        P(None, "freq", None, "src"),
        P(None, "src"),
        P(None, "freq", None, "src"),
        P("freq", "src"),
    )
    return jax.shard_map(
        local, mesh=mesh, in_specs=placed, out_specs=P(None, "freq", None, "src"), check_vma=False
    )
```

```python
import functools
import math

import jax
import jax.numpy as jnp
import numpy as np
from jax import lax
from jax.experimental import pallas as pl
from jax.experimental.pallas import tpu as pltpu
from jax.sharding import PartitionSpec as P

ITERS = 2
AHEAD = 4
TOGETHER = 2
CUTS = 2
TILE = 16
LANES = 128
MIB = 1024 * 1024
NT = (((1,), (1,)), ((), ()))
VMEM = pl.BlockSpec(memory_space=pltpu.VMEM)
BF = jnp.bfloat16
STAGES = (((1, 3), 38), ((0,), 36), ((2,), 32))
LIGHT = pl.CostEstimate(flops=1, bytes_accessed=1, transcendentals=0)


def mm(left, right):
    return jnp.dot(left, right, preferred_element_type=jnp.float32)


def nt(left, right):
    return lax.dot_general(left, right, NT, preferred_element_type=jnp.float32)


def tables(columns, rows, freq_local, focal_block):
    plane_devices = columns * rows
    half = plane_devices * focal_block
    nfreq = 2 * plane_devices * freq_local
    packed = half * freq_local * 2
    pack = np.zeros((packed, packed), np.float32)
    for xy in range(plane_devices):
        for j in range(focal_block):
            for f in range(freq_local):
                for c in range(2):
                    row = ((xy * focal_block + j) * freq_local + f) * 2 + c
                    pack[row, ((f * 2 + c) * plane_devices + xy) * focal_block + j] = 1
    positions = np.arange(nfreq)
    phase = (np.outer(positions, positions) % nfreq) * (2.0 * math.pi / nfreq)
    cosine, sine = np.cos(phase), np.sin(phase)
    to_time = np.zeros((2, nfreq, nfreq, 2))
    to_time[0, :, :, 0] = cosine / nfreq
    to_time[0, :, :, 1] = -sine / nfreq
    to_time[1, :, :, 0] = sine / nfreq
    to_time[1, :, :, 1] = cosine / nfreq
    to_freq = np.zeros((nfreq, 2, 2, nfreq))
    to_freq[:, 0, 0, :] = cosine
    to_freq[:, 0, 1, :] = sine
    to_freq[:, 1, 0, :] = -sine
    to_freq[:, 1, 1, :] = cosine
    to_time = to_time.reshape(2 * nfreq, columns, 2, rows, freq_local * 2).transpose(0, 1, 3, 2, 4)
    to_time = to_time.reshape(2 * nfreq, 2 * nfreq).astype(np.float32)
    to_freq = to_freq.reshape(2 * nfreq, 2 * nfreq).astype(np.float32)
    return pack, to_time, to_freq


def spread(wide_ref, update_ref):
    for slab in range(wide_ref.shape[0]):
        wide_ref[slab] = update_ref[:, slab * LANES : (slab + 1) * LANES].astype(jnp.float32)


def every(wide_ref, start, count, stride):
    slabs = [wide_ref[slab, pl.ds(start, count, stride), :] for slab in range(wide_ref.shape[0])]
    return jnp.concatenate(slabs, axis=1)


def wide(update):
    rows, width = update.shape
    return pltpu.VMEM((width // LANES, rows, LANES), jnp.float32)


def weights(polarity, half, block, freqs, initial_ref, wide_ref, left_ref, right_ref):
    _, nfreq, focal, width = initial_ref.shape
    for freq in freqs:
        planes = []
        for plane in range(2):
            value = initial_ref[plane, freq].astype(jnp.float32)
            if wide_ref is not None:
                value = value + every(wide_ref, 2 * freq + plane, focal, 2 * nfreq)
                value = value.astype(BF).astype(jnp.float32)
            value = value.reshape(focal // (2 * block), 2, block, width)
            planes.append([value[:, h].reshape(focal // 2, width) for h in range(2)])
        for place in range(2):
            real, imag = [jnp.where(half == place, low, high) for low, high in planes]
            here = slice(place * focal, (place + 1) * focal)
            left_ref[freq, :, here] = jnp.concatenate([real, imag], axis=0).T.astype(BF)
            right = jnp.concatenate([-polarity * imag, polarity * real], axis=0)
            right_ref[freq, :, here] = right.T.astype(BF)


def product_kernel(polarity, rels, build, tokens, focal_rows, blocks_shape, where_ref, reflection_ref, *refs):
    if build:
        source_ref, *refs = refs
    else:
        left_ref, right_ref, *refs = refs
    refs = refs[tokens:]
    outs, refs = refs[: len(rels)], refs[len(rels) :]
    held_ref, *refs = refs
    if build:
        left_ref, right_ref, *refs = refs
    sems, *refs = refs
    if build:
        initial_ref, initial_sem = refs
    nfreq, width, _ = outs[0].shape
    pieces = [(place, freq) for place in range(len(rels)) for freq in range(nfreq)]
    blocks = [jnp.bitwise_xor(where_ref[0], rel) for rel in rels]

    def fetch(piece, plane):
        place, freq = pieces[piece]
        return pltpu.make_async_copy(
            reflection_ref.at[plane, freq, pl.ds(blocks[place] * width, width), :],
            held_ref.at[piece, plane],
            sems.at[piece, plane],
        )

    def begin(piece):
        if piece < len(pieces):
            for plane in range(2):
                fetch(piece, plane).start()

    if build:
        load = pltpu.make_async_copy(source_ref, initial_ref, initial_sem)
        load.start()
    for piece in range(AHEAD):
        begin(piece)
    if build:
        load.wait()
        weights(polarity, where_ref[1], focal_rows, range(nfreq), initial_ref, None, left_ref, right_ref)

    source_blocks, receiver_blocks = blocks_shape
    strips = receiver_blocks // 4
    tall = width // strips
    wide_block = width // source_blocks

    def mask_of(place, strip):
        row = blocks[place] * strips + strip
        within = [where_ref[2 + column * receiver_blocks + row] for column in range(source_blocks)]
        parts = [jnp.full((TILE, wide_block), value.astype(jnp.float32)) for value in within]
        return jnp.concatenate(parts, axis=1).astype(BF)

    for low in range(0, len(pieces), TOGETHER):
        both = range(low, min(low + TOGETHER, len(pieces)))
        for piece in both:
            for plane in range(2):
                fetch(piece, plane).wait()
        for piece in both:
            begin(piece + AHEAD)
        for piece in both:
            place, freq = pieces[piece]
            masks = [mask_of(place, strip) for strip in range(strips)]
            masked = []
            for plane in range(2):
                parts = []
                for strip in range(strips):
                    part = held_ref[piece, plane, strip * tall : (strip + 1) * tall, :]
                    part = part.reshape(tall // TILE, TILE, width) * masks[strip][None]
                    parts.append(part.reshape(tall, width))
                masked.append(jnp.concatenate(parts, axis=0))
                held_ref[piece, plane] = masked[plane]
            total = mm(masked[0], left_ref[freq]) + mm(masked[1], right_ref[freq])
            outs[place][freq] = total.astype(BF)


def products(polarity, rels, focal_rows, limit, blocks, where, reflection, initial, built=None, after=()):
    planes, nfreq, receivers, sources = reflection.shape
    focal = initial.shape[2]
    out = jax.ShapeDtypeStruct((nfreq, sources, 2 * focal), BF)
    pieces = len(rels) * nfreq
    outs = [out] * len(rels) + [jax.ShapeDtypeStruct((pieces, planes, sources, sources), BF)]
    scratch = [pltpu.SemaphoreType.DMA((pieces, planes))]
    anywhere = pl.BlockSpec(memory_space=pl.ANY)
    smem = pl.BlockSpec(memory_space=pltpu.SMEM)
    build = built is None
    if build:
        outs += [out] * 2
        scratch += [pltpu.VMEM(initial.shape, BF), pltpu.SemaphoreType.DMA(())]
        extra, specs = [initial], [anywhere]
    else:
        extra, specs = list(built), [VMEM] * 2
    return pl.pallas_call(
        functools.partial(product_kernel, polarity, rels, build, len(after), focal_rows, blocks),
        in_specs=[smem, anywhere] + specs + [anywhere] * len(after),
        out_specs=[VMEM] * len(outs),
        scratch_shapes=scratch,
        out_shape=outs,
        compiler_params=pltpu.CompilerParams(vmem_limit_bytes=limit * MIB),
        cost_estimate=LIGHT,
        name="products",
    )(where, reflection, *extra, *after)


def product_again_kernel(polarity, build, tokens, focal_rows, where_ref, held_ref, *refs):
    if build:
        initial_ref, update_ref, *refs = refs
        refs = refs[tokens:]
        *outs, left_ref, right_ref, wide_ref = refs
        spread(wide_ref, update_ref)
    else:
        left_ref, right_ref, *refs = refs
        outs = refs[tokens:]
    nfreq = left_ref.shape[0]
    for freq in range(nfreq):
        if build:
            weights(polarity, where_ref[1], focal_rows, (freq,), initial_ref, wide_ref, left_ref, right_ref)
        for place, out_ref in enumerate(outs):
            piece = place * nfreq + freq
            total = mm(held_ref[piece, 0], left_ref[freq]) + mm(held_ref[piece, 1], right_ref[freq])
            out_ref[freq] = total.astype(BF)


def products_again(polarity, focal_rows, where, held, initial, update=None, built=None, after=()):
    _, nfreq, focal, sources = initial.shape
    build = built is None
    out = jax.ShapeDtypeStruct((nfreq, sources, 2 * focal), BF)
    extra = [initial, update] if build else list(built)
    outs = [out] * (held.shape[0] // nfreq + (2 if build else 0))
    return pl.pallas_call(
        functools.partial(product_again_kernel, polarity, build, len(after), focal_rows),
        in_specs=[pl.BlockSpec(memory_space=pltpu.SMEM)]
        + [VMEM] * (1 + len(extra))
        + [pl.BlockSpec(memory_space=pl.ANY)] * len(after),
        out_specs=[VMEM] * len(outs),
        scratch_shapes=[wide(update)] if build else [],
        out_shape=outs,
        compiler_params=pltpu.CompilerParams(vmem_limit_bytes=16 * MIB),
        cost_estimate=LIGHT,
        name="products_again",
    )(where, held, *extra, *after)


def call(kernel, name, outs, *args, after=()):
    return pl.pallas_call(
        kernel,
        in_specs=[VMEM] * len(args) + [pl.BlockSpec(memory_space=pl.ANY)] * len(after),
        out_specs=[VMEM] * len(outs),
        out_shape=[jax.ShapeDtypeStruct(shape, BF) for shape in outs],
        compiler_params=pltpu.CompilerParams(vmem_limit_bytes=16 * MIB),
        cost_estimate=LIGHT,
        name=name,
    )(*args, *after)


def add_kernel(place, tokens, mine_ref, core_ref, *refs):
    outs = refs[tokens:]
    lanes = outs[0].shape[2]
    here = slice(place * lanes, (place + 1) * lanes)
    low = 0
    for out_ref in outs:
        some = slice(low, low + out_ref.shape[1])
        low += out_ref.shape[1]
        total = mine_ref[:, some, here].astype(jnp.float32) + core_ref[:, some, here].astype(jnp.float32)
        out_ref[...] = total.astype(BF)


def total_kernel(index, pack_ref, mine_ref, core_ref, far_ref, *refs):
    out_ref = refs[-1]
    nfreq, count, lanes = far_ref.shape
    some = slice(index * count, (index + 1) * count)
    parts = []
    for f in range(nfreq):
        total = mine_ref[f, some, lanes:].astype(jnp.float32) + core_ref[f, some, lanes:].astype(jnp.float32)
        parts.append((total + far_ref[f].astype(jnp.float32)).astype(BF))
    packed = nt(pack_ref[...], jnp.concatenate(parts, axis=1))
    out_ref[...] = packed.reshape(out_ref.shape).astype(BF)


def pack_own_kernel(where_ref, pack_ref, mine_ref, core_ref, far_ref, *refs):
    *outer_refs, out_ref = refs
    nfreq, width, lanes = far_ref.shape
    group = 2 * nfreq
    mine = where_ref[1] == 0
    parts = []
    for f in range(nfreq):
        total = mine_ref[f, :, :lanes].astype(jnp.float32) + core_ref[f, :, :lanes].astype(jnp.float32)
        parts.append((total + far_ref[f].astype(jnp.float32)).astype(BF))
    own = nt(pack_ref[...], jnp.concatenate(parts, axis=1))
    outer = [ref[...].astype(jnp.float32).reshape(own.shape[0], ref.shape[2]) for ref in outer_refs]
    outer = jnp.concatenate(outer, axis=1)
    packed = [jnp.where(mine, own, outer), jnp.where(mine, outer, own)]
    packed = [part.reshape(part.shape[0] // group, group, width) for part in packed]
    out_ref[...] = jnp.stack(packed, axis=1).reshape(out_ref.shape).astype(BF)


def pack_own(where, shape, *args):
    return pl.pallas_call(
        pack_own_kernel,
        in_specs=[pl.BlockSpec(memory_space=pltpu.SMEM)] + [VMEM] * len(args),
        out_specs=VMEM,
        out_shape=jax.ShapeDtypeStruct(shape, BF),
        compiler_params=pltpu.CompilerParams(vmem_limit_bytes=16 * MIB),
        cost_estimate=LIGHT,
        name="pack_own",
    )(where, *args)


def window_kernel(dft_ref, onsets_ref, traces_ref, out_ref):
    focal, width = onsets_ref.shape
    devices, rows, _ = traces_ref.shape
    rows = rows // focal
    nfreq = dft_ref.shape[1] // 2
    step = lax.broadcasted_iota(jnp.int32, (nfreq, width), 0)
    results = []
    for j in range(focal):
        column = traces_ref[:, j * rows : (j + 1) * rows, :].reshape(2 * nfreq, width)
        time = mm(dft_ref[0], column)
        keep = step < onsets_ref[j : j + 1, :]
        keep = jnp.concatenate([keep, keep], axis=0)
        time = jnp.where(keep, time, 0.0).astype(BF)
        back = mm(dft_ref[1], time)
        results.append(back.reshape(2 * devices, rows // 2, width))
    out_ref[...] = jnp.stack(results, axis=1).reshape(out_ref.shape).astype(BF)


def final_kernel(initial_ref, update_ref, out_ref, wide_ref, block_ref, sems):
    planes, nfreq, focal, _ = initial_ref.shape
    spread(wide_ref, update_ref)
    copies = []
    for freq in range(nfreq):
        for plane in range(planes):
            value = initial_ref[plane, freq].astype(jnp.float32)
            value = value + every(wide_ref, planes * freq + plane, focal, planes * nfreq)
            block_ref[plane, freq] = value.astype(BF)
            copy = pltpu.make_async_copy(
                block_ref.at[plane, freq], out_ref.at[plane, freq], sems.at[plane, freq]
            )
            copy.start()
            copies.append(copy)
    for copy in copies:
        copy.wait()


def finish(initial, update):
    planes, nfreq, focal, sources = initial.shape
    return pl.pallas_call(
        final_kernel,
        in_specs=[VMEM, VMEM],
        out_specs=pl.BlockSpec(memory_space=pl.ANY),
        scratch_shapes=[
            wide(update),
            pltpu.VMEM(initial.shape, BF),
            pltpu.SemaphoreType.DMA((planes, nfreq)),
        ],
        out_shape=jax.ShapeDtypeStruct(initial.shape, BF),
        compiler_params=pltpu.CompilerParams(vmem_limit_bytes=16 * MIB),
        name="finish",
    )(initial, update)


def swap(values, bit):
    return lax.ppermute(values, "src", [(i, i ^ bit) for i in range(lax.axis_size("src"))])


def outward(values, columns, rows):
    pairs = []
    for x in range(columns):
        for h in range(2):
            for y in range(rows):
                for s in range(4):
                    here = ((x * 2 + h) * rows + y) * 4 + s
                    there = ((x * 2 + 1 - h) * rows + y) * 4 + (s ^ 2)
                    pairs.append((here, there))
    return lax.ppermute(values, ("freq", "src"), pairs)


def local(reflection, aperture, initial, onsets):
    planes, freq_local, receivers, sources = reflection.shape
    devices = lax.axis_size("freq")
    focal = initial.shape[2]
    focal_block = focal // devices
    columns = rows = math.isqrt(devices // 2)
    pack, to_time, to_freq = tables(columns, rows, freq_local, focal_block)
    pack = jnp.asarray(pack, BF)
    dft = jnp.asarray(np.stack([to_time, to_freq]), BF)
    half = (lax.axis_index("freq") // rows) % 2
    where = jnp.stack([lax.axis_index("src"), half]).astype(jnp.int32)
    where = jnp.concatenate([where, aperture.T.reshape(-1)])
    blocks = aperture.shape[::-1]
    plane_groups = [
        [(x * 2 + h) * rows + y for x in range(columns) for y in range(rows)] for h in range(2)
    ]
    block_rows = focal_block * freq_local * planes
    part = (freq_local, sources, focal)
    cut = (freq_local, sources // CUTS, focal)
    packed_cut = (devices // 2, block_rows, sources // CUTS)

    focal_rows = rows * focal_block
    held = []
    update = None
    for iteration in range(ITERS):
        polarity = 1.0 if iteration % 2 == 0 else -1.0

        def respond(stage, **more):
            if iteration:
                return products_again(polarity, focal_rows, where, held[stage], initial, **more)
            rels, limit = STAGES[stage]
            results = list(products(polarity, rels, focal_rows, limit, blocks, where, reflection, initial, **more))
            held.append(results.pop(len(rels)))
            return results

        first = {"update": update} if iteration else {}
        send_near, send_far, left, right = respond(0, **first)
        core_near, core_far = swap(send_near, 1), swap(send_far, 1)
        (near,) = respond(1, built=(left, right))
        totals = call(functools.partial(add_kernel, 1, 0), "add", [cut] * CUTS, near, core_near)
        far_other = [swap(total, 2) for total in totals]
        (remote,) = respond(2, built=(left, right), after=totals)
        (total,) = call(functools.partial(add_kernel, 0, 1), "add", [part], remote, core_far, after=far_other[:1])
        far_own = swap(total, 2)
        outer = []
        for index, far in enumerate(far_other):
            (other,) = call(
                functools.partial(total_kernel, index), "total", [packed_cut], pack, remote, core_far, far, after=(total,)
            )
            outer.append(outward(other, columns, rows))
        shape = (devices // 2, 2 * block_rows, sources)
        responses = pack_own(where, shape, pack, near, core_near, far_own, *outer)
        traces = lax.all_to_all(responses, "freq", 0, 0, tiled=True, axis_index_groups=plane_groups)
        (truncated,) = call(
            window_kernel, "window", [(devices, block_rows, sources)], dft, onsets, traces
        )
        update = lax.all_to_all(truncated, "freq", 0, 0, tiled=True)
        update = update.reshape(devices * block_rows, sources)
    return finish(initial, update)


def solution(mesh):
    placed = (
        P(None, "freq", None, "src"),
        P(None, "src"),
        P(None, "freq", None, "src"),
        P("freq", "src"),
    )
    return jax.shard_map(
        local, mesh=mesh, in_specs=placed, out_specs=P(None, "freq", None, "src"), check_vma=False
    )
```

```python
import functools
import math

import jax
import jax.numpy as jnp
import numpy as np
from jax import lax
from jax.experimental import pallas as pl
from jax.experimental.pallas import tpu as pltpu
from jax.sharding import PartitionSpec as P

ITERS = 2
AHEAD = 6
TOGETHER = 2
CUTS = 2
TILE = 16
LANES = 128
MIB = 1024 * 1024
NT = (((1,), (1,)), ((), ()))
VMEM = pl.BlockSpec(memory_space=pltpu.VMEM)
BF = jnp.bfloat16
STAGES = (((1, 3), 38), ((0,), 36), ((2,), 32))
LIGHT = pl.CostEstimate(flops=1, bytes_accessed=1, transcendentals=0)


def mm(left, right):
    return jnp.dot(left, right, preferred_element_type=jnp.float32)


def nt(left, right):
    return lax.dot_general(left, right, NT, preferred_element_type=jnp.float32)


def tables(columns, rows, freq_local, focal_block):
    plane_devices = columns * rows
    half = plane_devices * focal_block
    nfreq = 2 * plane_devices * freq_local
    packed = half * freq_local * 2
    pack = np.zeros((packed, packed), np.float32)
    for xy in range(plane_devices):
        for j in range(focal_block):
            for f in range(freq_local):
                for c in range(2):
                    row = ((xy * focal_block + j) * freq_local + f) * 2 + c
                    pack[row, ((f * 2 + c) * plane_devices + xy) * focal_block + j] = 1
    positions = np.arange(nfreq)
    phase = (np.outer(positions, positions) % nfreq) * (2.0 * math.pi / nfreq)
    cosine, sine = np.cos(phase), np.sin(phase)
    to_time = np.zeros((2, nfreq, nfreq, 2))
    to_time[0, :, :, 0] = cosine / nfreq
    to_time[0, :, :, 1] = -sine / nfreq
    to_time[1, :, :, 0] = sine / nfreq
    to_time[1, :, :, 1] = cosine / nfreq
    to_freq = np.zeros((nfreq, 2, 2, nfreq))
    to_freq[:, 0, 0, :] = cosine
    to_freq[:, 0, 1, :] = sine
    to_freq[:, 1, 0, :] = -sine
    to_freq[:, 1, 1, :] = cosine
    to_time = to_time.reshape(2 * nfreq, columns, 2, rows, freq_local * 2).transpose(0, 1, 3, 2, 4)
    to_time = to_time.reshape(2 * nfreq, 2 * nfreq).astype(np.float32)
    to_freq = to_freq.reshape(2 * nfreq, 2 * nfreq).astype(np.float32)
    return pack, to_time, to_freq


def spread(wide_ref, update_ref):
    for slab in range(wide_ref.shape[0]):
        wide_ref[slab] = update_ref[:, slab * LANES : (slab + 1) * LANES].astype(jnp.float32)


def every(wide_ref, start, count, stride):
    slabs = [wide_ref[slab, pl.ds(start, count, stride), :] for slab in range(wide_ref.shape[0])]
    return jnp.concatenate(slabs, axis=1)


def wide(update):
    rows, width = update.shape
    return pltpu.VMEM((width // LANES, rows, LANES), jnp.float32)


def weights(polarity, half, block, freqs, initial_ref, wide_ref, left_ref, right_ref):
    _, nfreq, focal, width = initial_ref.shape
    for freq in freqs:
        planes = []
        for plane in range(2):
            value = initial_ref[plane, freq].astype(jnp.float32)
            if wide_ref is not None:
                value = value + every(wide_ref, 2 * freq + plane, focal, 2 * nfreq)
                value = value.astype(BF).astype(jnp.float32)
            value = value.reshape(focal // (2 * block), 2, block, width)
            planes.append([value[:, h].reshape(focal // 2, width) for h in range(2)])
        for place in range(2):
            real, imag = [jnp.where(half == place, low, high) for low, high in planes]
            here = slice(place * focal, (place + 1) * focal)
            left_ref[freq, :, here] = jnp.concatenate([real, imag], axis=0).T.astype(BF)
            right = jnp.concatenate([-polarity * imag, polarity * real], axis=0)
            right_ref[freq, :, here] = right.T.astype(BF)


def product_kernel(polarity, rels, build, tokens, focal_rows, blocks_shape, where_ref, reflection_ref, *refs):
    if build:
        source_ref, *refs = refs
    else:
        left_ref, right_ref, *refs = refs
    refs = refs[tokens:]
    outs, refs = refs[: len(rels)], refs[len(rels) :]
    held_ref, *refs = refs
    if build:
        left_ref, right_ref, *refs = refs
    sems, *refs = refs
    if build:
        initial_ref, initial_sem = refs
    nfreq, width, _ = outs[0].shape
    pieces = [(place, freq) for place in range(len(rels)) for freq in range(nfreq)]
    blocks = [jnp.bitwise_xor(where_ref[0], rel) for rel in rels]

    def fetch(piece, plane):
        place, freq = pieces[piece]
        return pltpu.make_async_copy(
            reflection_ref.at[plane, freq, pl.ds(blocks[place] * width, width), :],
            held_ref.at[piece, plane],
            sems.at[piece, plane],
        )

    def begin(piece):
        if piece < len(pieces):
            for plane in range(2):
                fetch(piece, plane).start()

    if build:
        load = pltpu.make_async_copy(source_ref, initial_ref, initial_sem)
        load.start()
    for piece in range(AHEAD):
        begin(piece)
    if build:
        load.wait()
        weights(polarity, where_ref[1], focal_rows, range(nfreq), initial_ref, None, left_ref, right_ref)

    source_blocks, receiver_blocks = blocks_shape
    strips = receiver_blocks // 4
    tall = width // strips
    wide_block = width // source_blocks

    def mask_of(place, strip):
        row = blocks[place] * strips + strip
        within = [where_ref[2 + column * receiver_blocks + row] for column in range(source_blocks)]
        parts = [jnp.full((TILE, wide_block), value.astype(jnp.float32)) for value in within]
        return jnp.concatenate(parts, axis=1).astype(BF)

    for low in range(0, len(pieces), TOGETHER):
        both = range(low, min(low + TOGETHER, len(pieces)))
        for piece in both:
            for plane in range(2):
                fetch(piece, plane).wait()
        for piece in both:
            begin(piece + AHEAD)
        for piece in both:
            place, freq = pieces[piece]
            masks = [mask_of(place, strip) for strip in range(strips)]
            masked = []
            for plane in range(2):
                parts = []
                for strip in range(strips):
                    part = held_ref[piece, plane, strip * tall : (strip + 1) * tall, :]
                    part = part.reshape(tall // TILE, TILE, width) * masks[strip][None]
                    parts.append(part.reshape(tall, width))
                masked.append(jnp.concatenate(parts, axis=0))
                held_ref[piece, plane] = masked[plane]
            total = mm(masked[0], left_ref[freq]) + mm(masked[1], right_ref[freq])
            outs[place][freq] = total.astype(BF)


def products(polarity, rels, focal_rows, limit, blocks, where, reflection, initial, built=None, after=()):
    planes, nfreq, receivers, sources = reflection.shape
    focal = initial.shape[2]
    out = jax.ShapeDtypeStruct((nfreq, sources, 2 * focal), BF)
    pieces = len(rels) * nfreq
    outs = [out] * len(rels) + [jax.ShapeDtypeStruct((pieces, planes, sources, sources), BF)]
    scratch = [pltpu.SemaphoreType.DMA((pieces, planes))]
    anywhere = pl.BlockSpec(memory_space=pl.ANY)
    smem = pl.BlockSpec(memory_space=pltpu.SMEM)
    build = built is None
    if build:
        outs += [out] * 2
        scratch += [pltpu.VMEM(initial.shape, BF), pltpu.SemaphoreType.DMA(())]
        extra, specs = [initial], [anywhere]
    else:
        extra, specs = list(built), [VMEM] * 2
    return pl.pallas_call(
        functools.partial(product_kernel, polarity, rels, build, len(after), focal_rows, blocks),
        in_specs=[smem, anywhere] + specs + [anywhere] * len(after),
        out_specs=[VMEM] * len(outs),
        scratch_shapes=scratch,
        out_shape=outs,
        compiler_params=pltpu.CompilerParams(vmem_limit_bytes=limit * MIB),
        cost_estimate=LIGHT,
        name="products",
    )(where, reflection, *extra, *after)


def product_again_kernel(polarity, build, tokens, focal_rows, where_ref, held_ref, *refs):
    if build:
        initial_ref, update_ref, *refs = refs
        refs = refs[tokens:]
        *outs, left_ref, right_ref, wide_ref = refs
        spread(wide_ref, update_ref)
    else:
        left_ref, right_ref, *refs = refs
        outs = refs[tokens:]
    nfreq = left_ref.shape[0]
    for freq in range(nfreq):
        if build:
            weights(polarity, where_ref[1], focal_rows, (freq,), initial_ref, wide_ref, left_ref, right_ref)
        for place, out_ref in enumerate(outs):
            piece = place * nfreq + freq
            total = mm(held_ref[piece, 0], left_ref[freq]) + mm(held_ref[piece, 1], right_ref[freq])
            out_ref[freq] = total.astype(BF)


def products_again(polarity, focal_rows, where, held, initial, update=None, built=None, after=()):
    _, nfreq, focal, sources = initial.shape
    build = built is None
    out = jax.ShapeDtypeStruct((nfreq, sources, 2 * focal), BF)
    extra = [initial, update] if build else list(built)
    outs = [out] * (held.shape[0] // nfreq + (2 if build else 0))
    return pl.pallas_call(
        functools.partial(product_again_kernel, polarity, build, len(after), focal_rows),
        in_specs=[pl.BlockSpec(memory_space=pltpu.SMEM)]
        + [VMEM] * (1 + len(extra))
        + [pl.BlockSpec(memory_space=pl.ANY)] * len(after),
        out_specs=[VMEM] * len(outs),
        scratch_shapes=[wide(update)] if build else [],
        out_shape=outs,
        compiler_params=pltpu.CompilerParams(vmem_limit_bytes=16 * MIB),
        cost_estimate=LIGHT,
        name="products_again",
    )(where, held, *extra, *after)


def call(kernel, name, outs, *args, after=()):
    return pl.pallas_call(
        kernel,
        in_specs=[VMEM] * len(args) + [pl.BlockSpec(memory_space=pl.ANY)] * len(after),
        out_specs=[VMEM] * len(outs),
        out_shape=[jax.ShapeDtypeStruct(shape, BF) for shape in outs],
        compiler_params=pltpu.CompilerParams(vmem_limit_bytes=16 * MIB),
        cost_estimate=LIGHT,
        name=name,
    )(*args, *after)


def add_kernel(place, tokens, mine_ref, core_ref, *refs):
    outs = refs[tokens:]
    lanes = outs[0].shape[2]
    here = slice(place * lanes, (place + 1) * lanes)
    low = 0
    for out_ref in outs:
        some = slice(low, low + out_ref.shape[1])
        low += out_ref.shape[1]
        total = mine_ref[:, some, here].astype(jnp.float32) + core_ref[:, some, here].astype(jnp.float32)
        out_ref[...] = total.astype(BF)


def total_kernel(index, pack_ref, mine_ref, core_ref, far_ref, *refs):
    out_ref = refs[-1]
    nfreq, count, lanes = far_ref.shape
    some = slice(index * count, (index + 1) * count)
    parts = []
    for f in range(nfreq):
        total = mine_ref[f, some, lanes:].astype(jnp.float32) + core_ref[f, some, lanes:].astype(jnp.float32)
        parts.append((total + far_ref[f].astype(jnp.float32)).astype(BF))
    packed = nt(pack_ref[...], jnp.concatenate(parts, axis=1))
    out_ref[...] = packed.reshape(out_ref.shape).astype(BF)


def pack_own_kernel(where_ref, pack_ref, mine_ref, core_ref, far_ref, *refs):
    *outer_refs, out_ref = refs
    nfreq, width, lanes = far_ref.shape
    group = 2 * nfreq
    mine = where_ref[1] == 0
    parts = []
    for f in range(nfreq):
        total = mine_ref[f, :, :lanes].astype(jnp.float32) + core_ref[f, :, :lanes].astype(jnp.float32)
        parts.append((total + far_ref[f].astype(jnp.float32)).astype(BF))
    own = nt(pack_ref[...], jnp.concatenate(parts, axis=1))
    outer = [ref[...].astype(jnp.float32).reshape(own.shape[0], ref.shape[2]) for ref in outer_refs]
    outer = jnp.concatenate(outer, axis=1)
    packed = [jnp.where(mine, own, outer), jnp.where(mine, outer, own)]
    packed = [part.reshape(part.shape[0] // group, group, width) for part in packed]
    out_ref[...] = jnp.stack(packed, axis=1).reshape(out_ref.shape).astype(BF)


def pack_own(where, shape, *args):
    return pl.pallas_call(
        pack_own_kernel,
        in_specs=[pl.BlockSpec(memory_space=pltpu.SMEM)] + [VMEM] * len(args),
        out_specs=VMEM,
        out_shape=jax.ShapeDtypeStruct(shape, BF),
        compiler_params=pltpu.CompilerParams(vmem_limit_bytes=16 * MIB),
        cost_estimate=LIGHT,
        name="pack_own",
    )(where, *args)


def window_kernel(dft_ref, onsets_ref, traces_ref, out_ref):
    focal, width = onsets_ref.shape
    devices, rows, _ = traces_ref.shape
    rows = rows // focal
    nfreq = dft_ref.shape[1] // 2
    step = lax.broadcasted_iota(jnp.int32, (nfreq, width), 0)
    results = []
    for j in range(focal):
        column = traces_ref[:, j * rows : (j + 1) * rows, :].reshape(2 * nfreq, width)
        time = mm(dft_ref[0], column)
        keep = step < onsets_ref[j : j + 1, :]
        keep = jnp.concatenate([keep, keep], axis=0)
        time = jnp.where(keep, time, 0.0).astype(BF)
        back = mm(dft_ref[1], time)
        results.append(back.reshape(2 * devices, rows // 2, width))
    out_ref[...] = jnp.stack(results, axis=1).reshape(out_ref.shape).astype(BF)


def final_kernel(initial_ref, update_ref, out_ref, wide_ref, block_ref, sems):
    planes, nfreq, focal, _ = initial_ref.shape
    spread(wide_ref, update_ref)
    copies = []
    for freq in range(nfreq):
        for plane in range(planes):
            value = initial_ref[plane, freq].astype(jnp.float32)
            value = value + every(wide_ref, planes * freq + plane, focal, planes * nfreq)
            block_ref[plane, freq] = value.astype(BF)
            copy = pltpu.make_async_copy(
                block_ref.at[plane, freq], out_ref.at[plane, freq], sems.at[plane, freq]
            )
            copy.start()
            copies.append(copy)
    for copy in copies:
        copy.wait()


def finish(initial, update):
    planes, nfreq, focal, sources = initial.shape
    return pl.pallas_call(
        final_kernel,
        in_specs=[VMEM, VMEM],
        out_specs=pl.BlockSpec(memory_space=pl.ANY),
        scratch_shapes=[
            wide(update),
            pltpu.VMEM(initial.shape, BF),
            pltpu.SemaphoreType.DMA((planes, nfreq)),
        ],
        out_shape=jax.ShapeDtypeStruct(initial.shape, BF),
        compiler_params=pltpu.CompilerParams(vmem_limit_bytes=16 * MIB),
        name="finish",
    )(initial, update)


def swap(values, bit):
    return lax.ppermute(values, "src", [(i, i ^ bit) for i in range(lax.axis_size("src"))])


def outward(values, columns, rows):
    pairs = []
    for x in range(columns):
        for h in range(2):
            for y in range(rows):
                for s in range(4):
                    here = ((x * 2 + h) * rows + y) * 4 + s
                    there = ((x * 2 + 1 - h) * rows + y) * 4 + (s ^ 2)
                    pairs.append((here, there))
    return lax.ppermute(values, ("freq", "src"), pairs)


def local(reflection, aperture, initial, onsets):
    planes, freq_local, receivers, sources = reflection.shape
    devices = lax.axis_size("freq")
    focal = initial.shape[2]
    focal_block = focal // devices
    columns = rows = math.isqrt(devices // 2)
    pack, to_time, to_freq = tables(columns, rows, freq_local, focal_block)
    pack = jnp.asarray(pack, BF)
    dft = jnp.asarray(np.stack([to_time, to_freq]), BF)
    half = (lax.axis_index("freq") // rows) % 2
    where = jnp.stack([lax.axis_index("src"), half]).astype(jnp.int32)
    where = jnp.concatenate([where, aperture.T.reshape(-1)])
    blocks = aperture.shape[::-1]
    plane_groups = [
        [(x * 2 + h) * rows + y for x in range(columns) for y in range(rows)] for h in range(2)
    ]
    block_rows = focal_block * freq_local * planes
    part = (freq_local, sources, focal)
    cut = (freq_local, sources // CUTS, focal)
    packed_cut = (devices // 2, block_rows, sources // CUTS)

    focal_rows = rows * focal_block
    held = []
    update = None
    for iteration in range(ITERS):
        polarity = 1.0 if iteration % 2 == 0 else -1.0

        def respond(stage, **more):
            if iteration:
                return products_again(polarity, focal_rows, where, held[stage], initial, **more)
            rels, limit = STAGES[stage]
            results = list(products(polarity, rels, focal_rows, limit, blocks, where, reflection, initial, **more))
            held.append(results.pop(len(rels)))
            return results

        first = {"update": update} if iteration else {}
        send_near, send_far, left, right = respond(0, **first)
        core_near, core_far = swap(send_near, 1), swap(send_far, 1)
        (near,) = respond(1, built=(left, right))
        totals = call(functools.partial(add_kernel, 1, 0), "add", [cut] * CUTS, near, core_near)
        far_other = [swap(total, 2) for total in totals]
        (remote,) = respond(2, built=(left, right), after=totals)
        (total,) = call(functools.partial(add_kernel, 0, 1), "add", [part], remote, core_far, after=far_other[:1])
        far_own = swap(total, 2)
        outer = []
        for index, far in enumerate(far_other):
            (other,) = call(
                functools.partial(total_kernel, index), "total", [packed_cut], pack, remote, core_far, far, after=(total,)
            )
            outer.append(outward(other, columns, rows))
        shape = (devices // 2, 2 * block_rows, sources)
        responses = pack_own(where, shape, pack, near, core_near, far_own, *outer)
        traces = lax.all_to_all(responses, "freq", 0, 0, tiled=True, axis_index_groups=plane_groups)
        (truncated,) = call(
            window_kernel, "window", [(devices, block_rows, sources)], dft, onsets, traces
        )
        update = lax.all_to_all(truncated, "freq", 0, 0, tiled=True)
        update = update.reshape(devices * block_rows, sources)
    return finish(initial, update)


def solution(mesh):
    placed = (
        P(None, "freq", None, "src"),
        P(None, "src"),
        P(None, "freq", None, "src"),
        P("freq", "src"),
    )
    return jax.shard_map(
        local, mesh=mesh, in_specs=placed, out_specs=P(None, "freq", None, "src"), check_vma=False
    )
```
